512 devices in a mesh: seq: 64 (over y, z), tp: 8 (over x, core).
Axes of the slice: x: 4, y: 4, z: 16, core: 2. Of those that a mesh axis runs over, the one named last changes fastest.
Arguments:
- queries: bfloat16 [16384, 8, 8, 128], P('seq', None, 'tp'), may hold values from -6 to 6
- keys: bfloat16 [16384, 8, 128], P('seq'), may hold values from -6 to 6
- values: bfloat16 [16384, 8, 128], P('seq'), may hold values from -6 to 6
- grad_out: bfloat16 [16384, 8, 8, 128], P('seq', None, 'tp'), may hold values from -6 to 6
- exponents: int32 [128, 8, 8], P('seq', None, 'tp'), may hold values from -2 to 2
- lengths: int32 [128], replicated, may hold values from 1 to 256, 16384 in all
Outputs:
- grad_queries: bfloat16 [16384, 8, 8, 128], P('seq', None, 'tp')
- grad_keys: bfloat16 [16384, 8, 128], P('seq', 'tp')
- grad_values: bfloat16 [16384, 8, 128], P('seq', 'tp')
The draws below stay inside these ranges and needn't reach their ends.
Inputs may be any that keep to these rules, and one draw needn't show every extreme that they name: No document has more than 256 tokens (at least one has exactly 256); the lengths sum to 16384. `exponents`: one exponent for each block of 128 tokens of one query head.
All inputs are finite; a program needn't handle non-finite values.
Results may differ from the reference program's by a relative error of at most 0.03.
Values may be sent and summed in bfloat16 or wider, within the bound.
No kernel may reach another device: no remote copies, remote signals or barrier semaphores. Data moves between devices by JAX's collectives and lax.ppermute only.
A program may use at most 64 MiB of HBM per device.

```python
import math
import jax
import jax.numpy as jnp
import numpy as np
from jax import lax

G = 8
HD = 128
R = 8
TOK_DEV = 256
EB = 128
TOKENS = 16384
DOCS = 128


def draw_queries(key, part):
    key = jax.random.fold_in(key, 11)
    result = jnp.clip(jax.random.normal(key, (TOKENS, G, R, HD), jnp.float32), -6.0, 6.0)
    return result.astype(jnp.bfloat16)


def draw_keys(key, part):
    key = jax.random.fold_in(key, 12)
    result = jnp.clip(jax.random.normal(key, (TOKENS, G, HD), jnp.float32), -6.0, 6.0)
    return result.astype(jnp.bfloat16)


def plant(values, stream_key, low, high):
    longest = values.shape.index(max(values.shape))
    spots = []
    for shift in (0, 1):
        where = [jax.random.randint(jax.random.fold_in(stream_key, axis), (), 0, length) for axis, length in enumerate(values.shape)]
        where[longest] = (where[longest] + shift) % values.shape[longest]
        spots.append(tuple(where))
    return values.at[spots[0]].set(low).at[spots[1]].set(high)


def block_levels(stream_key, extent, cuts, smallest, top_value):
    loudness, own = 1.0, jax.random.fold_in(stream_key, 6)
    for dim, shards_of in cuts:
        steps = jnp.exp(jax.random.uniform(jax.random.fold_in(own, dim), (shards_of,), jnp.float32, smallest / len(cuts), top_value / len(cuts)))
        loudness = loudness * jnp.repeat(steps, extent[dim] // shards_of).reshape([-1 if axis == dim else 1 for axis in range(len(extent))])
    return loudness


def split_up(number_of, total, bound, skew):
    weights = [(1 << 20) // math.isqrt(standing ** skew) + 1 for standing in range(2, number_of + 1)]
    rest, counts = total - bound - (number_of - 1), [1] * (number_of - 1)
    while rest > 0:
        movable = [i for i in range(number_of - 1) if counts[i] < bound]
        mass, budget = sum([weights[i] for i in movable]), rest
        for i in movable:
            more = min(bound - counts[i], max(1, budget * weights[i] // mass), rest)
            counts[i] = counts[i] + more
            rest = rest - more
    return np.array([bound] + counts)


def ragged_sizes(own_key, amount, total, limit, lean):
    if amount == 2:
        one = jax.random.randint(own_key, (), max(1, total - limit), min(limit, total - 1) + 1)
        return jnp.stack([one, total - one])
    sizes = jnp.asarray(split_up(amount, total, limit, lean), jnp.int32)
    twos = (amount - 1) // 2
    source_of, receiver = sizes[1:1 + 2 * twos:2], sizes[2:2 + 2 * twos:2]
    margin = jnp.minimum(source_of - 1, limit - receiver)
    moved = jax.random.randint(jax.random.fold_in(own_key, 1), (twos,), 0, 1 << 20) % (margin + 1)
    sizes = sizes.at[1:1 + 2 * twos:2].set(source_of - moved).at[2:2 + 2 * twos:2].set(receiver + moved)
    return sizes[jax.random.permutation(jax.random.fold_in(own_key, 2), amount)]


def normal_values(rng, shape, width, most, pieces=(), kind=jnp.bfloat16):
    array = width * jax.random.normal(rng, shape, jnp.float32)
    if pieces:
        array = array * block_levels(rng, shape, pieces, -0.22, 0.18)
    return jnp.clip(array, -most, most).astype(kind)


def setup_inputs(seed: int = 0) -> dict:
    streams_of = jax.random.split(jax.random.key(seed), 7)
    queries = draw_queries(jax.random.fold_in(streams_of[6], 71), 0)
    keys = draw_keys(jax.random.fold_in(streams_of[6], 71), 0)
    values = normal_values(streams_of[2], (TOKENS, G, HD), 1.0, 6.0, ((0, 64),))
    grad_out = normal_values(streams_of[3], (TOKENS, G, R, HD), 1.0, 6.0, ((0, 64), (2, 8)))
    exponents = plant(jax.random.randint(streams_of[4], (TOKENS // EB, G, R), -2, 3), jax.random.fold_in(streams_of[4], 1), -2, 2).astype(jnp.int32)
    lengths = ragged_sizes(streams_of[5], DOCS, TOKENS, TOK_DEV, 1).astype(jnp.int32)
    return {"queries": queries, "keys": keys, "values": values, "grad_out": grad_out, "exponents": exponents, "lengths": lengths}


def doc_numbers(lengths, positions):
    doc_ends = jnp.cumsum(lengths).astype(jnp.int32)
    return jnp.sum((doc_ends[None, :] <= positions[:, None]).astype(jnp.int32), axis=1)


def block_grads(query_blk, dout_blk, key_window, value_window, allowed, scaling):
    query_f = query_blk.astype(jnp.float32)
    dout_f = dout_blk.astype(jnp.float32)
    key_f = key_window.astype(jnp.float32)
    value_f = value_window.astype(jnp.float32)
    scores = jnp.einsum('qgrd,kgd->grqk', query_f, key_f) * scaling
    scores = jnp.where(allowed[None, None], scores, -1e30)
    row_max = jnp.max(scores, axis=-1, keepdims=True)
    shifted = jnp.exp(scores - row_max)
    row_sum = jnp.sum(shifted, axis=-1, keepdims=True)
    attn_w = shifted / row_sum
    attn_low = lax.optimization_barrier(attn_w.astype(jnp.bfloat16)).astype(jnp.float32)
    attn_out = jnp.einsum('grqk,kgd->qgrd', attn_low, value_f).astype(jnp.bfloat16)
    attn_out = lax.optimization_barrier(attn_out).astype(jnp.float32)
    row_delta = jnp.transpose(jnp.sum(dout_f * attn_out, axis=-1), (1, 2, 0))[..., None]
    grad_probs = jnp.einsum('qgrd,kgd->grqk', dout_f, value_f)
    grad_scores = (scaling * attn_w * (grad_probs - row_delta)).astype(jnp.bfloat16)
    grad_scores = lax.optimization_barrier(grad_scores).astype(jnp.float32)
    grad_query = jnp.einsum('grqk,kgd->qgrd', grad_scores, key_f).astype(jnp.bfloat16)
    grad_key = jnp.einsum('grqk,qgrd->kgd', grad_scores, query_f)
    grad_value = jnp.einsum('grqk,qgrd->kgd', attn_low, dout_f)
    return grad_query, grad_key, grad_value


def reference(queries, keys, values, grad_out, exponents, lengths):
    token_count = queries.shape[0]
    block_count = token_count // TOK_DEV
    scaling = HD ** -0.5
    factor = jnp.exp2(exponents.astype(jnp.float32))
    scaled = grad_out.reshape(token_count // EB, EB, G, R, HD).astype(jnp.float32) * factor[:, None, :, :, None]
    scaled = scaled.astype(jnp.bfloat16).reshape(token_count, G, R, HD)
    padding = jnp.zeros((TOK_DEV, G, HD), keys.dtype)
    key_padded = jnp.concatenate([padding, keys], axis=0)
    value_padded = jnp.concatenate([padding, values], axis=0)

    def one_block(block_index):
        start = (block_index * TOK_DEV).astype(jnp.int32)
        query_blk = lax.dynamic_slice_in_dim(queries, start, TOK_DEV, 0)
        dout_blk = lax.dynamic_slice_in_dim(scaled, start, TOK_DEV, 0)
        key_window = lax.dynamic_slice_in_dim(key_padded, start, 2 * TOK_DEV, 0)
        value_window = lax.dynamic_slice_in_dim(value_padded, start, 2 * TOK_DEV, 0)
        query_pos = start + jnp.arange(TOK_DEV, dtype=jnp.int32)
        key_pos = start - TOK_DEV + jnp.arange(2 * TOK_DEV, dtype=jnp.int32)
        query_doc = doc_numbers(lengths, query_pos)
        key_doc = doc_numbers(lengths, key_pos)
        allowed = (query_doc[:, None] == key_doc[None, :]) & (key_pos[None, :] <= query_pos[:, None]) & (key_pos[None, :] >= 0)
        return block_grads(query_blk, dout_blk, key_window, value_window, allowed, scaling)

    grad_query, key_terms, value_terms = lax.map(one_block, jnp.arange(block_count, dtype=jnp.int32))
    tail = jnp.zeros((1, TOK_DEV, G, HD), key_terms.dtype)
    grad_keys = key_terms[:, TOK_DEV:] + jnp.concatenate([key_terms[1:, :TOK_DEV], tail], axis=0)
    grad_values = value_terms[:, TOK_DEV:] + jnp.concatenate([value_terms[1:, :TOK_DEV], tail], axis=0)
    grad_queries = grad_query.reshape(token_count, G, R, HD)
    return (grad_queries,
            grad_keys.astype(jnp.bfloat16).reshape(token_count, G, HD),
            grad_values.astype(jnp.bfloat16).reshape(token_count, G, HD))
```

```python
import functools
import math

import jax
import jax.numpy as jnp
from jax import lax
from jax.experimental import pallas as pl
from jax.experimental.pallas import tpu as pltpu
from jax.sharding import PartitionSpec as P

BF16 = jnp.bfloat16
F32 = jnp.float32
MASKED = -1e30
VMEM = pl.BlockSpec(memory_space=pltpu.VMEM)
SMEM = pl.BlockSpec(memory_space=pltpu.SMEM)


def params():
    return pltpu.CompilerParams(vmem_limit_bytes=40 * 1024 * 1024)


def dot_nt(a, b):
    return lax.dot_general(a, b, (((1,), (1,)), ((), ())), preferred_element_type=F32)


def dot_nn(a, b):
    return lax.dot_general(a, b, (((1,), (0,)), ((), ())), preferred_element_type=F32)


def shifted(block, axis, distance):
    size = lax.axis_size(axis)
    route = [(i - distance, i) for i in range(size) if 0 <= i - distance < size]
    return lax.ppermute(block, axis, route)


def fill_bias(bias, lengths_ref, first_row):
    keys, rows = bias.shape
    docs = lengths_ref.shape[1]
    lengths = lengths_ref[...]
    i = lax.broadcasted_iota(jnp.int32, (docs, docs), 0)
    j = lax.broadcasted_iota(jnp.int32, (docs, docs), 1)
    ends = jnp.sum(jnp.where(j <= i, lengths, 0), axis=1, keepdims=True) - first_row
    t = lax.broadcasted_iota(jnp.int32, (docs, rows), 1)
    start = jnp.max(jnp.where(ends <= t, ends, -first_row), axis=0, keepdims=True)
    u = lax.broadcasted_iota(jnp.int32, (keys, rows), 0) - (keys - rows)
    t = lax.broadcasted_iota(jnp.int32, (keys, rows), 1)
    bias[...] = jnp.where((u <= t) & (u >= start), 0.0, MASKED).astype(F32)


def pair_terms(query, dout, key, value, bias, scaling):
    scores = dot_nt(key, query) * (scaling * math.log2(math.e)) + bias
    shifted_exp = jnp.exp2(scores - jnp.max(scores, axis=0, keepdims=True))
    probs = shifted_exp * (1.0 / jnp.sum(shifted_exp, axis=0, keepdims=True))
    grad_probs = dot_nt(value, dout)
    row_delta = jnp.sum(probs * grad_probs, axis=0, keepdims=True)
    return probs.astype(BF16), (probs * (grad_probs - row_delta)).astype(BF16)


def prepare_kernel(query_ref, grad_ref, key_ref, value_ref, exp_ref, qd_ref, kv_ref):
    blocks, groups = exp_ref.shape
    rows = grad_ref.shape[0] // blocks
    kv_ref[0] = jnp.swapaxes(key_ref[...], 0, 1)
    kv_ref[1] = jnp.swapaxes(value_ref[...], 0, 1)
    qd_ref[:, 0] = jnp.swapaxes(query_ref[...], 0, 1)
    factor = jnp.exp2(exp_ref[...].astype(F32)).astype(BF16)
    for b in range(blocks):
        part = pl.ds(b * rows, rows)
        qd_ref[:, 1, part] = jnp.swapaxes(grad_ref[part], 0, 1) * factor[b][:, None, None]


def key_side_kernel(scaling, where_ref, lengths_ref, qd_ref, back_ref, here_ref, cross_ref, own_ref, bias, key, value, dkey, dvalue):
    rows = here_ref.shape[2]
    fill_bias(bias, lengths_ref, where_ref[0])
    key[:rows] = back_ref[0, 0]
    key[rows:] = here_ref[0, 0]
    value[:rows] = back_ref[1, 0]
    value[rows:] = here_ref[1, 0]
    for h in range(qd_ref.shape[0]):
        query, dout = qd_ref[h, 0], qd_ref[h, 1]
        probs, grad_scores = pair_terms(query, dout, key[...], value[...], bias[...], scaling)
        if h == 0:
            dvalue[...] = dot_nn(probs, dout)
            dkey[...] = dot_nn(grad_scores, query)
        else:
            dvalue[...] += dot_nn(probs, dout)
            dkey[...] += dot_nn(grad_scores, query)
    cross_ref[0] = (dkey[:rows] * scaling).astype(BF16)
    cross_ref[1] = dvalue[:rows].astype(BF16)
    own_ref[0] = dkey[rows:] * scaling
    own_ref[1] = dvalue[rows:]


def query_side_kernel(scaling, where_ref, lengths_ref, qd_ref, back_ref, here_ref, out_ref, bias, grads):
    fill_bias(bias, lengths_ref, where_ref[0])
    for g in range(qd_ref.shape[0]):
        key = jnp.concatenate([back_ref[0, g], here_ref[0, g]], axis=0)
        value = jnp.concatenate([back_ref[1, g], here_ref[1, g]], axis=0)
        _, grad_scores = pair_terms(qd_ref[g, 0], qd_ref[g, 1], key, value, bias[...], scaling)
        grads[g] = (dot_nn(key.T, grad_scores) * scaling).astype(BF16).T
    out_ref[...] = jnp.swapaxes(grads[...], 0, 1)


def finish_kernel(own_ref, back_ref, key_ref, value_ref):
    key_ref[...] = (own_ref[0] + back_ref[0].astype(F32)).astype(BF16)
    value_ref[...] = (own_ref[1] + back_ref[1].astype(F32)).astype(BF16)


def per_device(queries, keys, values, grad_out, exponents, lengths):
    rows, groups, _, width = queries.shape
    scaling = width ** (-0.5)
    shape = jax.ShapeDtypeStruct
    where = jnp.stack([lax.axis_index("seq") * rows, lax.axis_index("tp")]).astype(jnp.int32)
    lengths = lengths.reshape(1, -1)
    qd, kv = pl.pallas_call(
        prepare_kernel,
        in_specs=[VMEM] * 5,
        out_specs=[VMEM] * 2,
        out_shape=[shape((groups, 2, rows, width), BF16), shape((2, groups, rows, width), BF16)],
        compiler_params=params(),
    )(
        queries.reshape(rows, groups, width),
        grad_out.reshape(rows, groups, width),
        keys,
        values,
        exponents.reshape(-1, groups),
    )
    kv_back = shifted(kv, "seq", 1)
    qd_group = lax.all_to_all(qd, "tp", split_axis=0, concat_axis=0, tiled=True)
    whole = lambda i, where: (0, 0)
    one_group = pl.BlockSpec((2, 1, rows, width), lambda i, where: (0, where[1], 0, 0))
    pairs = qd.shape[0]
    flops = 2 * 2 * rows * rows * width * pairs
    cross, own = pl.pallas_call(
        functools.partial(key_side_kernel, scaling),
        grid_spec=pltpu.PrefetchScalarGridSpec(
            num_scalar_prefetch=1,
            grid=(1,),
            in_specs=[
                pl.BlockSpec(lengths.shape, whole),
                pl.BlockSpec(qd_group.shape, lambda i, where: (0, 0, 0, 0)),
                one_group,
                one_group,
            ],
            out_specs=[pl.BlockSpec((2, rows, width), lambda i, where: (0, 0, 0))] * 2,
            scratch_shapes=[
                pltpu.VMEM((2 * rows, rows), F32),
                pltpu.VMEM((2 * rows, width), BF16),
                pltpu.VMEM((2 * rows, width), BF16),
                pltpu.VMEM((2 * rows, width), F32),
                pltpu.VMEM((2 * rows, width), F32),
            ],
        ),
        out_shape=[shape((2, rows, width), BF16), shape((2, rows, width), F32)],
        compiler_params=params(),
        cost_estimate=pl.CostEstimate(flops=4 * flops, bytes_accessed=2**21, transcendentals=2 * rows * rows * pairs),
    )(where, lengths, qd_group, kv_back, kv)
    back = shifted(cross, "seq", -1)
    grad_queries = pl.pallas_call(
        functools.partial(query_side_kernel, scaling),
        in_specs=[SMEM] + [VMEM] * 4,
        out_specs=VMEM,
        out_shape=shape((rows, groups, width), BF16),
        scratch_shapes=[pltpu.VMEM((2 * rows, rows), F32), pltpu.VMEM((groups, rows, width), BF16)],
        compiler_params=params(),
        cost_estimate=pl.CostEstimate(flops=3 * flops, bytes_accessed=2**22, transcendentals=2 * rows * rows * pairs),
    )(where, lengths, qd, kv_back, kv)
    grad_keys, grad_values = pl.pallas_call(
        finish_kernel,
        in_specs=[VMEM] * 2,
        out_specs=[VMEM] * 2,
        out_shape=[shape((rows, width), BF16)] * 2,
        compiler_params=params(),
    )(own, back)
    return (
        grad_queries.reshape(queries.shape),
        grad_keys.reshape(rows, 1, width),
        grad_values.reshape(rows, 1, width),
    )


def solution(mesh):
    placed = (
        P("seq", None, "tp", None),
        P("seq", None, None),
        P("seq", None, None),
        P("seq", None, "tp", None),
        P("seq", None, "tp"),
        P(),
    )
    return jax.shard_map(
        per_device,
        mesh=mesh,
        in_specs=placed,
        out_specs=(P("seq", None, "tp", None), P("seq", "tp", None), P("seq", "tp", None)),
        check_vma=False,
    )
```

```python
import functools
import math

import jax
import jax.numpy as jnp
from jax import lax
from jax.experimental import pallas as pl
from jax.experimental.pallas import tpu as pltpu
from jax.sharding import PartitionSpec as P

BF16 = jnp.bfloat16
F32 = jnp.float32
MASKED = -1e30
VMEM = pl.BlockSpec(memory_space=pltpu.VMEM)
SMEM = pl.BlockSpec(memory_space=pltpu.SMEM)


def params():
    return pltpu.CompilerParams(vmem_limit_bytes=40 * 1024 * 1024)


def dot_nt(a, b):
    return lax.dot_general(a, b, (((1,), (1,)), ((), ())), preferred_element_type=F32)


def dot_nn(a, b):
    return lax.dot_general(a, b, (((1,), (0,)), ((), ())), preferred_element_type=F32)


def shifted(block, axis, distance):
    size = lax.axis_size(axis)
    route = [(i - distance, i) for i in range(size) if 0 <= i - distance < size]
    return lax.ppermute(block, axis, route)


def fill_bias(bias, lengths_ref, first_row):
    keys, rows = bias.shape
    half = rows // 2
    docs = lengths_ref.shape[1]
    lengths = lengths_ref[...]
    i = lax.broadcasted_iota(jnp.int32, (docs, docs), 0)
    j = lax.broadcasted_iota(jnp.int32, (docs, docs), 1)
    ends = jnp.sum(jnp.where(j <= i, lengths, 0), axis=1, keepdims=True) - first_row
    t = lax.broadcasted_iota(jnp.int32, (docs, rows), 1)
    start = jnp.max(jnp.where(ends <= t, ends, -first_row), axis=0, keepdims=True)
    row = lax.broadcasted_iota(jnp.int32, (keys, rows), 0)
    t = lax.broadcasted_iota(jnp.int32, (keys, rows), 1)
    u = jnp.where((row >= rows) & (t < half), row - 2 * rows, row - half)
    bias[...] = jnp.where((u <= t) & (u >= start), 0.0, MASKED).astype(F32)


def window_dots(keys, queries):
    rows = queries.shape[0]
    half = rows // 2
    middle = dot_nt(keys[half : half + rows], queries)
    corners = jnp.concatenate(
        [dot_nt(keys[:half], queries[:half]), dot_nt(keys[half + rows :], queries[half:])], axis=1
    )
    return middle, corners


def pair_terms(query, dout, key, value, bias, scaling):
    rows = query.shape[0]
    fold = scaling * math.log2(math.e)
    middle, corners = window_dots(key, query)
    middle = middle * fold + bias[:rows]
    corners = corners * fold + bias[rows:]
    row_max = jnp.maximum(jnp.max(middle, axis=0, keepdims=True), jnp.max(corners, axis=0, keepdims=True))
    middle = jnp.exp2(middle - row_max)
    corners = jnp.exp2(corners - row_max)
    inverse = 1.0 / (jnp.sum(middle, axis=0, keepdims=True) + jnp.sum(corners, axis=0, keepdims=True))
    middle = middle * inverse
    corners = corners * inverse
    grad_middle, grad_corners = window_dots(value, dout)
    row_delta = jnp.sum(middle * grad_middle, axis=0, keepdims=True) + jnp.sum(
        corners * grad_corners, axis=0, keepdims=True
    )
    return (
        middle.astype(BF16),
        corners.astype(BF16),
        (middle * (grad_middle - row_delta)).astype(BF16),
        (corners * (grad_corners - row_delta)).astype(BF16),
    )


def query_prepare_kernel(query_ref, grad_ref, exp_ref, qd_ref):
    blocks, groups = exp_ref.shape
    rows = grad_ref.shape[0] // blocks
    qd_ref[:, 0] = jnp.swapaxes(query_ref[...], 0, 1)
    factor = jnp.exp2(exp_ref[...].astype(F32)).astype(BF16)
    for b in range(blocks):
        part = pl.ds(b * rows, rows)
        qd_ref[:, 1, part] = jnp.swapaxes(grad_ref[part], 0, 1) * factor[b][:, None, None]


def key_prepare_kernel(key_ref, value_ref, kv_ref):
    kv_ref[0] = jnp.swapaxes(key_ref[...], 0, 1)
    kv_ref[1] = jnp.swapaxes(value_ref[...], 0, 1)


def window_prepare_kernel(where_ref, here_ref, other_ref, kv_ref):
    core = where_ref[1] % 2
    kv_ref[core] = jnp.swapaxes(here_ref[...], 0, 1)
    kv_ref[1 - core] = jnp.swapaxes(other_ref[...], 0, 1)


def query_side_kernel(scaling, where_ref, lengths_ref, qd_ref, back_ref, here_ref, out_ref, bias, grads):
    fill_bias(bias, lengths_ref, where_ref[0])
    rows = qd_ref.shape[2]
    half = rows // 2
    for g in range(qd_ref.shape[0]):
        key = jnp.concatenate([back_ref[0, g], here_ref[0, g]], axis=0)
        value = jnp.concatenate([back_ref[1, g], here_ref[1, g]], axis=0)
        _, _, middle, corners = pair_terms(qd_ref[g, 0], qd_ref[g, 1], key, value, bias[...], scaling)
        key_t = key.T
        total = dot_nn(key_t[:, half : half + rows], middle) + jnp.concatenate(
            [dot_nn(key_t[:, :half], corners[:, :half]), dot_nn(key_t[:, half + rows :], corners[:, half:])],
            axis=1,
        )
        grads[g] = (total * scaling).astype(BF16).T
    out_ref[...] = jnp.swapaxes(grads[...], 0, 1)


def key_side_kernel(scaling, where_ref, lengths_ref, qd_ref, back_ref, here_ref, cross_ref, own_ref, bias, mid_terms, left_terms, right_terms):
    heads, _, rows, width = qd_ref.shape
    half = rows // 2
    fill_bias(bias, lengths_ref, where_ref[0])
    key = jnp.concatenate([back_ref[0, 0], here_ref[0, 0]], axis=0)
    value = jnp.concatenate([back_ref[1, 0], here_ref[1, 0]], axis=0)
    for h in range(heads):
        probs, probs_c, grads, grads_c = pair_terms(qd_ref[h, 0], qd_ref[h, 1], key, value, bias[...], scaling)
        at, at_half = pl.ds(h * rows, rows), pl.ds(h * half, half)
        mid_terms[0, :, at] = grads
        mid_terms[1, :, at] = probs
        left_terms[0, :, at_half] = grads_c[:, :half]
        left_terms[1, :, at_half] = probs_c[:, :half]
        right_terms[0, :, at_half] = grads_c[:, half:]
        right_terms[1, :, at_half] = probs_c[:, half:]
    for i, factor in ((0, scaling), (1, 1.0)):
        both = qd_ref[:, i].reshape(heads * rows, width)
        early = qd_ref[:, i, :half].reshape(heads * half, width)
        late = qd_ref[:, i, half:].reshape(heads * half, width)
        middle = dot_nn(mid_terms[i], both) * factor
        cross_ref[i, :half] = (dot_nn(left_terms[i], early) * factor).astype(BF16)
        cross_ref[i, half:] = middle[:half].astype(BF16)
        own_ref[i, :half] = middle[half:]
        own_ref[i, half:] = dot_nn(right_terms[i], late) * factor


def finish_kernel(own_ref, back_ref, key_ref, value_ref):
    key_ref[...] = (own_ref[0] + back_ref[0].astype(F32)).astype(BF16)
    value_ref[...] = (own_ref[1] + back_ref[1].astype(F32)).astype(BF16)


def per_device(queries, keys, values, grad_out, exponents, lengths):
    rows, groups, _, width = queries.shape
    scaling = width ** (-0.5)
    shape = jax.ShapeDtypeStruct
    device = lax.axis_index("tp")
    where = jnp.stack([lax.axis_index("seq") * rows, device]).astype(jnp.int32)
    lengths = lengths.reshape(1, -1)
    pairs = 8
    flops = 2 * 2 * rows * rows * width * pairs
    bias = pltpu.VMEM((rows + rows // 2, rows), F32)

    def call(kernel, operands, out_shape, scratch=(), scalars=0, dots=0):
        many = isinstance(out_shape, list)
        return pl.pallas_call(
            kernel,
            in_specs=[SMEM] * scalars + [VMEM] * (len(operands) - scalars),
            out_specs=[VMEM] * len(out_shape) if many else VMEM,
            out_shape=out_shape,
            scratch_shapes=list(scratch),
            compiler_params=params(),
            cost_estimate=pl.CostEstimate(flops=flops * dots + 10**6, bytes_accessed=2**20, transcendentals=0),
            name=(kernel.func if isinstance(kernel, functools.partial) else kernel).__name__,
        )(*operands)

    half_kv = jnp.where(device % 2 == 0, keys, values)
    half_back = shifted(half_kv, "seq", 1)
    queries_3d = queries.reshape(rows, groups, width)
    queries_3d, half_kv = lax.optimization_barrier((queries_3d, half_kv))
    qd = call(
        query_prepare_kernel,
        (queries_3d, grad_out.reshape(rows, groups, width), exponents.reshape(-1, groups)),
        shape((groups, 2, rows, width), BF16),
    )
    qd_group = lax.all_to_all(qd, "tp", split_axis=0, concat_axis=0, tiled=True)
    kv_shape = shape((2, groups, rows, width), BF16)
    kv = call(key_prepare_kernel, (keys, values), kv_shape)
    other_half = lax.ppermute(half_back, "tp", [(d, d ^ 1) for d in range(lax.axis_size("tp"))])
    kv_back = call(window_prepare_kernel, (where, half_back, other_half), kv_shape, scalars=1)
    grad_queries = call(
        functools.partial(query_side_kernel, scaling),
        (where, lengths, qd, kv_back, kv),
        shape((rows, groups, width), BF16),
        [bias, pltpu.VMEM((groups, rows, width), BF16)],
        scalars=1,
        dots=3,
    )
    grad_queries, kv_back = lax.optimization_barrier((grad_queries, kv_back))
    whole = lambda i, where: (0, 0)
    one_group = pl.BlockSpec((2, 1, rows, width), lambda i, where: (0, where[1], 0, 0))
    cross, own = pl.pallas_call(
        functools.partial(key_side_kernel, scaling),
        grid_spec=pltpu.PrefetchScalarGridSpec(
            num_scalar_prefetch=1,
            grid=(1,),
            in_specs=[
                pl.BlockSpec(lengths.shape, whole),
                pl.BlockSpec(qd_group.shape, lambda i, where: (0, 0, 0, 0)),
                one_group,
                one_group,
            ],
            out_specs=[pl.BlockSpec((2, rows, width), lambda i, where: (0, 0, 0))] * 2,
            scratch_shapes=[
                bias,
                pltpu.VMEM((2, rows, pairs * rows), BF16),
                pltpu.VMEM((2, rows // 2, pairs * rows // 2), BF16),
                pltpu.VMEM((2, rows // 2, pairs * rows // 2), BF16),
            ],
        ),
        out_shape=[shape((2, rows, width), BF16), shape((2, rows, width), F32)],
        compiler_params=params(),
        cost_estimate=pl.CostEstimate(flops=4 * flops, bytes_accessed=2**21, transcendentals=0),
        name="key_side_kernel",
    )(where, lengths, qd_group, kv_back, kv)
    back = shifted(cross, "seq", -1)
    grad_keys, grad_values = call(finish_kernel, (own, back), [shape((rows, width), BF16)] * 2)
    return (
        grad_queries.reshape(queries.shape),
        grad_keys.reshape(rows, 1, width),
        grad_values.reshape(rows, 1, width),
    )


def solution(mesh):
    placed = (
        P("seq", None, "tp", None),
        P("seq", None, None),
        P("seq", None, None),
        P("seq", None, "tp", None),
        P("seq", None, "tp"),
        P(),
    )
    return jax.shard_map(
        per_device,
        mesh=mesh,
        in_specs=placed,
        out_specs=(P("seq", None, "tp", None), P("seq", "tp", None), P("seq", "tp", None)),
        check_vma=False,
    )
```

```python
import functools
import math

import jax
import jax.numpy as jnp
from jax import lax
from jax.experimental import pallas as pl
from jax.experimental.pallas import tpu as pltpu
from jax.sharding import PartitionSpec as P

BF16 = jnp.bfloat16
F32 = jnp.float32
MASKED = -1e30
VMEM = pl.BlockSpec(memory_space=pltpu.VMEM)
SMEM = pl.BlockSpec(memory_space=pltpu.SMEM)


def params():
    return pltpu.CompilerParams(vmem_limit_bytes=16 * 1024 * 1024)


def dot_nt(a, b):
    return lax.dot_general(a, b, (((1,), (1,)), ((), ())), preferred_element_type=F32)


def dot_nn(a, b):
    return lax.dot_general(a, b, (((1,), (0,)), ((), ())), preferred_element_type=F32)


def shifted(block, axis, distance):
    size = lax.axis_size(axis)
    route = [(i - distance, i) for i in range(size) if 0 <= i - distance < size]
    return lax.ppermute(block, axis, route)


def fill_bias(bias, lengths_ref, first_row):
    keys, rows = bias.shape
    half = rows // 2
    docs = lengths_ref.shape[1]
    lengths = lengths_ref[...]
    i = lax.broadcasted_iota(jnp.int32, (docs, docs), 0)
    j = lax.broadcasted_iota(jnp.int32, (docs, docs), 1)
    ends = jnp.sum(jnp.where(j <= i, lengths, 0), axis=1, keepdims=True) - first_row
    t = lax.broadcasted_iota(jnp.int32, (docs, rows), 1)
    start = jnp.max(jnp.where(ends <= t, ends, -first_row), axis=0, keepdims=True)
    row = lax.broadcasted_iota(jnp.int32, (keys, rows), 0)
    t = lax.broadcasted_iota(jnp.int32, (keys, rows), 1)
    u = jnp.where((row >= rows) & (t < half), row - 2 * rows, row - half)
    bias[...] = jnp.where((u <= t) & (u >= start), 0.0, MASKED).astype(F32)


def window_dots(keys, queries):
    rows = queries.shape[0]
    half = rows // 2
    middle = dot_nt(keys[half : half + rows], queries)
    corners = jnp.concatenate(
        [dot_nt(keys[:half], queries[:half]), dot_nt(keys[half + rows :], queries[half:])], axis=1
    )
    return middle, corners


def pair_terms(query, dout, key, value, bias, scaling):
    rows = query.shape[0]
    fold = scaling * math.log2(math.e)
    middle, corners = window_dots(key, query)
    middle = middle * fold + bias[:rows]
    corners = corners * fold + bias[rows:]
    row_max = jnp.maximum(jnp.max(middle, axis=0, keepdims=True), jnp.max(corners, axis=0, keepdims=True))
    middle = jnp.exp2(middle - row_max)
    corners = jnp.exp2(corners - row_max)
    inverse = 1.0 / (jnp.sum(middle, axis=0, keepdims=True) + jnp.sum(corners, axis=0, keepdims=True))
    middle = middle * inverse
    corners = corners * inverse
    grad_middle, grad_corners = window_dots(value, dout)
    row_delta = jnp.sum(middle * grad_middle, axis=0, keepdims=True) + jnp.sum(
        corners * grad_corners, axis=0, keepdims=True
    )
    return (
        middle.astype(BF16),
        corners.astype(BF16),
        (middle * (grad_middle - row_delta)).astype(BF16),
        (corners * (grad_corners - row_delta)).astype(BF16),
    )


def query_prepare_kernel(exp_ref, query_ref, grad_ref, qd_ref):
    qd_ref[:, 0] = jnp.swapaxes(query_ref[...], 0, 1)
    blocks, groups = exp_ref.shape
    rows = grad_ref.shape[0] // blocks
    factor = jnp.exp2(exp_ref[...].astype(F32)).astype(BF16)
    for b in range(blocks):
        part = pl.ds(b * rows, rows)
        qd_ref[:, 1, part] = jnp.swapaxes(grad_ref[part], 0, 1) * factor[b][:, None, None]


def key_prepare_kernel(where_ref, lengths_ref, key_ref, value_ref, kv_ref, bias_ref):
    fill_bias(bias_ref, lengths_ref, where_ref[0])
    kv_ref[0] = jnp.swapaxes(key_ref[...], 0, 1)
    kv_ref[1] = jnp.swapaxes(value_ref[...], 0, 1)


def query_grads(scaling, g, qd_ref, back_ref, kv_ref, bias_ref):
    rows = qd_ref.shape[2]
    half = rows // 2
    key = jnp.concatenate([back_ref[0, g], kv_ref[0, g]], axis=0)
    value = jnp.concatenate([back_ref[1, g], kv_ref[1, g]], axis=0)
    _, _, middle, corners = pair_terms(qd_ref[g, 0], qd_ref[g, 1], key, value, bias_ref[...], scaling)
    key_t = key.T
    total = dot_nn(key_t[:, half : half + rows], middle) + jnp.concatenate(
        [dot_nn(key_t[:, :half], corners[:, :half]), dot_nn(key_t[:, half + rows :], corners[:, half:])],
        axis=1,
    )
    return (total * scaling).astype(BF16).T


def early_query_kernel(scaling, where_ref, bias_ref, here_ref, other_ref, kv_ref, qd_ref, out_ref, back_ref):
    even = where_ref[1] % 2 == 0
    for g in range(here_ref.shape[0]):
        here, other = here_ref[g], other_ref[g]
        back_ref[0, g] = jnp.where(even, here, other)
        back_ref[1, g] = jnp.where(even, other, here)
    for g in range(out_ref.shape[0]):
        out_ref[g] = query_grads(scaling, g, qd_ref, back_ref, kv_ref, bias_ref)


def late_query_kernel(scaling, bias_ref, back_ref, kv_ref, early_ref, qd_ref, out_ref, grads):
    first, last = early_ref.shape[0], qd_ref.shape[0]
    grads[:first] = early_ref[...]
    for g in range(first, last):
        grads[g] = query_grads(scaling, g, qd_ref, back_ref, kv_ref, bias_ref)
    out_ref[...] = jnp.swapaxes(grads[...], 0, 1)


def key_side_kernel(
    scaling, where_ref, bias, qd_ref, back_ref, here_ref, cross_ref, own_ref, mid_terms, left_terms, right_terms
):
    heads, _, rows, width = qd_ref.shape
    half = rows // 2
    key = jnp.concatenate([back_ref[0, 0], here_ref[0, 0]], axis=0)
    value = jnp.concatenate([back_ref[1, 0], here_ref[1, 0]], axis=0)
    for h in range(heads):
        probs, probs_c, grads, grads_c = pair_terms(qd_ref[h, 0], qd_ref[h, 1], key, value, bias[...], scaling)
        at, at_half = pl.ds(h * rows, rows), pl.ds(h * half, half)
        mid_terms[0, :, at] = grads
        mid_terms[1, :, at] = probs
        left_terms[0, :, at_half] = grads_c[:, :half]
        left_terms[1, :, at_half] = probs_c[:, :half]
        right_terms[0, :, at_half] = grads_c[:, half:]
        right_terms[1, :, at_half] = probs_c[:, half:]
    for i, factor in ((0, scaling), (1, 1.0)):
        both = qd_ref[:, i].reshape(heads * rows, width)
        early = qd_ref[:, i, :half].reshape(heads * half, width)
        late = qd_ref[:, i, half:].reshape(heads * half, width)
        middle = dot_nn(mid_terms[i], both) * factor
        cross_ref[i, :half] = (dot_nn(left_terms[i], early) * factor).astype(BF16)
        cross_ref[i, half:] = middle[:half].astype(BF16)
        own_ref[i, :half] = middle[half:]
        own_ref[i, half:] = dot_nn(right_terms[i], late) * factor


def finish_kernel(own_ref, back_ref, key_ref, value_ref):
    key_ref[...] = (own_ref[0] + back_ref[0].astype(F32)).astype(BF16)
    value_ref[...] = (own_ref[1] + back_ref[1].astype(F32)).astype(BF16)


def per_device(queries, keys, values, grad_out, exponents, lengths):
    rows, groups, _, width = queries.shape
    scaling = width ** (-0.5)
    shape = jax.ShapeDtypeStruct
    device = lax.axis_index("tp")
    where = jnp.stack([lax.axis_index("seq") * rows, device]).astype(jnp.int32)
    lengths = lengths.reshape(1, -1)
    pairs = 8
    flops = 2 * 2 * rows * rows * width * pairs

    def call(kernel, operands, out_shape, scratch=(), first=VMEM, dots=0):
        many = isinstance(out_shape, list)
        return pl.pallas_call(
            kernel,
            in_specs=[first] + [VMEM] * (len(operands) - 1),
            out_specs=[VMEM] * len(out_shape) if many else VMEM,
            out_shape=out_shape,
            scratch_shapes=list(scratch),
            compiler_params=params(),
            cost_estimate=pl.CostEstimate(flops=flops * dots + 10**6, bytes_accessed=2**20, transcendentals=0),
            name=(kernel.func if isinstance(kernel, functools.partial) else kernel).__name__,
        )(*operands)

    half_kv = jnp.swapaxes(jnp.where(device % 2 == 0, keys, values), 0, 1)
    exponents = exponents.reshape(-1, groups)
    here = shifted(half_kv, "seq", 1)
    queries, half_kv = lax.optimization_barrier((queries, half_kv))
    qd = call(
        query_prepare_kernel,
        (exponents, queries.reshape(rows, groups, width), grad_out.reshape(rows, groups, width)),
        shape((groups, 2, rows, width), BF16),
    )
    qd_group = lax.all_to_all(qd, "tp", split_axis=0, concat_axis=0, tiled=True)
    kv_shape = shape((2, groups, rows, width), BF16)
    kv, bias = call(
        key_prepare_kernel,
        (where, lengths, keys, values),
        [kv_shape, shape((rows + rows // 2, rows), F32)],
        first=SMEM,
    )
    other = lax.ppermute(here, "tp", [(d, d ^ 1) for d in range(lax.axis_size("tp"))])
    early, back_kv = call(
        functools.partial(early_query_kernel, scaling),
        (where, bias, here, other, kv, qd),
        [shape((3, rows, width), BF16), kv_shape],
        dots=1,
        first=SMEM,
    )
    one_group = pl.BlockSpec((2, 1, rows, width), lambda i, where: (0, where[1], 0, 0))
    cross, own = pl.pallas_call(
        functools.partial(key_side_kernel, scaling),
        grid_spec=pltpu.PrefetchScalarGridSpec(
            num_scalar_prefetch=1,
            grid=(1,),
            in_specs=[
                pl.BlockSpec(bias.shape, lambda i, where: (0, 0)),
                pl.BlockSpec(qd_group.shape, lambda i, where: (0, 0, 0, 0)),
                one_group,
                one_group,
            ],
            out_specs=[pl.BlockSpec((2, rows, width), lambda i, where: (0, 0, 0))] * 2,
            scratch_shapes=[
                pltpu.VMEM((2, rows, pairs * rows), BF16),
                pltpu.VMEM((2, rows // 2, pairs * rows // 2), BF16),
                pltpu.VMEM((2, rows // 2, pairs * rows // 2), BF16),
            ],
        ),
        out_shape=[shape((2, rows, width), BF16), shape((2, rows, width), F32)],
        compiler_params=params(),
        cost_estimate=pl.CostEstimate(flops=4 * flops, bytes_accessed=2**21, transcendentals=0),
        name="key_side_kernel",
    )(where, bias, qd_group, back_kv, kv)
    back = shifted(cross, "seq", -1)
    grad_queries = call(
        functools.partial(late_query_kernel, scaling),
        (bias, back_kv, kv, early, qd),
        shape((rows, groups, width), BF16),
        [pltpu.VMEM((groups, rows, width), BF16)],
        dots=3,
    )
    grad_keys, grad_values = call(finish_kernel, (own, back), [shape((rows, width), BF16)] * 2)
    return (
        grad_queries.reshape(queries.shape),
        grad_keys.reshape(rows, 1, width),
        grad_values.reshape(rows, 1, width),
    )


def solution(mesh):
    placed = (
        P("seq", None, "tp", None),
        P("seq", None, None),
        P("seq", None, None),
        P("seq", None, "tp", None),
        P("seq", None, "tp"),
        P(),
    )
    return jax.shard_map(
        per_device,
        mesh=mesh,
        in_specs=placed,
        out_specs=(P("seq", None, "tp", None), P("seq", "tp", None), P("seq", "tp", None)),
        check_vma=False,
    )
```

```python
import functools
import math

import jax
import jax.numpy as jnp
from jax import lax
from jax.experimental import pallas as pl
from jax.experimental.pallas import tpu as pltpu
from jax.sharding import PartitionSpec as P

BF16 = jnp.bfloat16
F32 = jnp.float32
MASKED = -1e30
VMEM = pl.BlockSpec(memory_space=pltpu.VMEM)
SMEM = pl.BlockSpec(memory_space=pltpu.SMEM)


def params():
    return pltpu.CompilerParams(vmem_limit_bytes=16 * 1024 * 1024)


def dot_nt(a, b):
    return lax.dot_general(a, b, (((1,), (1,)), ((), ())), preferred_element_type=F32)


def dot_nn(a, b):
    return lax.dot_general(a, b, (((1,), (0,)), ((), ())), preferred_element_type=F32)


def shifted(block, axis, distance):
    size = lax.axis_size(axis)
    route = [(i - distance, i) for i in range(size) if 0 <= i - distance < size]
    return lax.ppermute(block, axis, route)


def fill_bias(bias, lengths_ref, first_row):
    keys, rows = bias.shape
    half = rows // 2
    docs = lengths_ref.shape[1]
    lengths = lengths_ref[...]
    i = lax.broadcasted_iota(jnp.int32, (docs, docs), 0)
    j = lax.broadcasted_iota(jnp.int32, (docs, docs), 1)
    ends = jnp.sum(jnp.where(j <= i, lengths, 0), axis=1, keepdims=True) - first_row
    t = lax.broadcasted_iota(jnp.int32, (docs, rows), 1)
    start = jnp.max(jnp.where(ends <= t, ends, -first_row), axis=0, keepdims=True)
    row = lax.broadcasted_iota(jnp.int32, (keys, rows), 0)
    t = lax.broadcasted_iota(jnp.int32, (keys, rows), 1)
    u = jnp.where((row >= rows) & (t < half), row - 2 * rows, row - half)
    bias[...] = jnp.where((u <= t) & (u >= start), 0.0, MASKED).astype(F32)


def window_dots(keys, queries):
    rows = queries.shape[0]
    half = rows // 2
    middle = dot_nt(keys[half : half + rows], queries)
    corners = jnp.concatenate(
        [dot_nt(keys[:half], queries[:half]), dot_nt(keys[half + rows :], queries[half:])], axis=1
    )
    return middle, corners


def pair_terms(query, dout, key, value, bias, scaling):
    rows = query.shape[0]
    fold = scaling * math.log2(math.e)
    middle, corners = window_dots(key, query)
    middle = middle * fold + bias[:rows]
    corners = corners * fold + bias[rows:]
    row_max = jnp.maximum(jnp.max(middle, axis=0, keepdims=True), jnp.max(corners, axis=0, keepdims=True))
    middle = jnp.exp2(middle - row_max)
    corners = jnp.exp2(corners - row_max)
    inverse = 1.0 / (jnp.sum(middle, axis=0, keepdims=True) + jnp.sum(corners, axis=0, keepdims=True))
    middle = middle * inverse
    corners = corners * inverse
    grad_middle, grad_corners = window_dots(value, dout)
    row_delta = jnp.sum(middle * grad_middle, axis=0, keepdims=True) + jnp.sum(
        corners * grad_corners, axis=0, keepdims=True
    )
    return (
        middle.astype(BF16),
        corners.astype(BF16),
        (middle * (grad_middle - row_delta)).astype(BF16),
        (corners * (grad_corners - row_delta)).astype(BF16),
    )


def query_prepare_kernel(exp_ref, query_ref, grad_ref, qd_ref):
    qd_ref[:, 0] = jnp.swapaxes(query_ref[...], 0, 1)
    blocks, groups = exp_ref.shape
    rows = grad_ref.shape[0] // blocks
    factor = jnp.exp2(exp_ref[...].astype(F32)).astype(BF16)
    for b in range(blocks):
        part = pl.ds(b * rows, rows)
        qd_ref[:, 1, part] = jnp.swapaxes(grad_ref[part], 0, 1) * factor[b][:, None, None]


def key_prepare_kernel(where_ref, lengths_ref, key_ref, value_ref, kv_ref, bias_ref, bias):
    fill_bias(bias, lengths_ref, where_ref[0])
    bias_ref[...] = bias[...].astype(BF16)
    kv_ref[0] = jnp.swapaxes(key_ref[...], 0, 1)
    kv_ref[1] = jnp.swapaxes(value_ref[...], 0, 1)


def query_grads(scaling, query, dout, key, value, bias):
    rows = query.shape[0]
    half = rows // 2
    _, _, middle, corners = pair_terms(query, dout, key, value, bias, scaling)
    key_t = key.T
    total = dot_nn(key_t[:, half : half + rows], middle) + jnp.concatenate(
        [dot_nn(key_t[:, :half], corners[:, :half]), dot_nn(key_t[:, half + rows :], corners[:, half:])],
        axis=1,
    )
    return (total * scaling).astype(BF16).T


def early_query_kernel(scaling, where_ref, bias_ref, here_ref, other_ref, kv_ref, qd_ref, stash_ref):
    d = where_ref[1]
    even = d % 2 == 0
    groups = here_ref.shape[0]
    early = (4 + 4 * groups - stash_ref.shape[0]) // 3
    bias = bias_ref[...].astype(F32)

    def window(g):
        here, other = here_ref[g], other_ref[g]
        return jnp.where(even, here, other), kv_ref[0, g], jnp.where(even, other, here), kv_ref[1, g]

    for i, part in enumerate(window(d)):
        stash_ref[i] = part
    for g in range(early, groups):
        for i, part in enumerate(window(g)):
            stash_ref[4 + early + 4 * (g - early) + i] = part
    for g in range(early):
        key_back, key, value_back, value = window(g)
        stash_ref[4 + g] = query_grads(
            scaling,
            qd_ref[g, 0],
            qd_ref[g, 1],
            jnp.concatenate([key_back, key], axis=0),
            jnp.concatenate([value_back, value], axis=0),
            bias,
        )


def late_query_kernel(scaling, bias_ref, stash_ref, qd_ref, out_ref, grads):
    groups, rows, _ = grads.shape
    late = qd_ref.shape[0]
    early = groups - late
    grads[:early] = stash_ref[4 : 4 + early]
    bias = bias_ref[...].astype(F32)
    for i in range(late):
        at = 4 + early + 4 * i
        key = stash_ref[at : at + 2].reshape(2 * rows, -1)
        value = stash_ref[at + 2 : at + 4].reshape(2 * rows, -1)
        grads[early + i] = query_grads(scaling, qd_ref[i, 0], qd_ref[i, 1], key, value, bias)
    out_ref[...] = jnp.swapaxes(grads[...], 0, 1)


def key_side_kernel(
    scaling, bias_ref, qd_ref, window_ref, cross_ref, own_ref, mid_terms, left_terms, right_terms
):
    heads, _, rows, width = qd_ref.shape
    half = rows // 2
    key = window_ref[:2].reshape(2 * rows, width)
    value = window_ref[2:].reshape(2 * rows, width)
    bias = bias_ref[...].astype(F32)
    for h in range(heads):
        probs, probs_c, grads, grads_c = pair_terms(qd_ref[h, 0], qd_ref[h, 1], key, value, bias, scaling)
        at, at_half = pl.ds(h * rows, rows), pl.ds(h * half, half)
        mid_terms[0, :, at] = grads
        mid_terms[1, :, at] = probs
        left_terms[0, :, at_half] = grads_c[:, :half]
        left_terms[1, :, at_half] = probs_c[:, :half]
        right_terms[0, :, at_half] = grads_c[:, half:]
        right_terms[1, :, at_half] = probs_c[:, half:]
    for i, factor in ((0, scaling), (1, 1.0)):
        both = qd_ref[:, i].reshape(heads * rows, width)
        early = qd_ref[:, i, :half].reshape(heads * half, width)
        late = qd_ref[:, i, half:].reshape(heads * half, width)
        middle = dot_nn(mid_terms[i], both) * factor
        cross_ref[i, :half] = (dot_nn(left_terms[i], early) * factor).astype(BF16)
        cross_ref[i, half:] = middle[:half].astype(BF16)
        own_ref[i, :half] = middle[half:]
        own_ref[i, half:] = dot_nn(right_terms[i], late) * factor


def finish_kernel(own_ref, back_ref, key_ref, value_ref):
    key_ref[...] = (own_ref[0] + back_ref[0].astype(F32)).astype(BF16)
    value_ref[...] = (own_ref[1] + back_ref[1].astype(F32)).astype(BF16)


def per_device(queries, keys, values, grad_out, exponents, lengths):
    rows, groups, _, width = queries.shape
    scaling = width ** (-0.5)
    shape = jax.ShapeDtypeStruct
    device = lax.axis_index("tp")
    where = jnp.stack([lax.axis_index("seq") * rows, device]).astype(jnp.int32)
    lengths = lengths.reshape(1, -1)
    pairs = 8
    flops = 2 * 2 * rows * rows * width * pairs

    def call(kernel, operands, out_shape, scratch=(), first=VMEM, dots=0):
        many = isinstance(out_shape, list)
        return pl.pallas_call(
            kernel,
            in_specs=[first] + [VMEM] * (len(operands) - 1),
            out_specs=[VMEM] * len(out_shape) if many else VMEM,
            out_shape=out_shape,
            scratch_shapes=list(scratch),
            compiler_params=params(),
            cost_estimate=pl.CostEstimate(flops=flops * dots + 10**6, bytes_accessed=2**20, transcendentals=0),
            name=(kernel.func if isinstance(kernel, functools.partial) else kernel).__name__,
        )(*operands)

    half_kv = jnp.swapaxes(jnp.where(device % 2 == 0, keys, values), 0, 1)
    exponents = exponents.reshape(-1, groups)
    here = shifted(half_kv, "seq", 1)
    queries, half_kv = lax.optimization_barrier((queries, half_kv))
    qd = call(
        query_prepare_kernel,
        (exponents, queries.reshape(rows, groups, width), grad_out.reshape(rows, groups, width)),
        shape((groups, 2, rows, width), BF16),
    )
    qd_group = lax.all_to_all(qd, "tp", split_axis=0, concat_axis=0, tiled=True)
    kv_shape = shape((2, groups, rows, width), BF16)
    bias_shape = (rows + rows // 2, rows)
    kv, bias = call(
        key_prepare_kernel,
        (where, lengths, keys, values),
        [kv_shape, shape(bias_shape, BF16)],
        [pltpu.VMEM(bias_shape, F32)],
        first=SMEM,
    )
    other = lax.ppermute(here, "tp", [(d, d ^ 1) for d in range(lax.axis_size("tp"))])
    late = 2
    early = groups - late
    stash = call(
        functools.partial(early_query_kernel, scaling),
        (where, bias, here, other, kv, qd),
        shape((4 + early + 4 * late, rows, width), BF16),
        dots=1,
        first=SMEM,
    )
    cross, own = pl.pallas_call(
        functools.partial(key_side_kernel, scaling),
        grid=(1,),
        in_specs=[
            pl.BlockSpec(bias.shape, lambda i: (0, 0)),
            pl.BlockSpec(qd_group.shape, lambda i: (0, 0, 0, 0)),
            pl.BlockSpec((4, rows, width), lambda i: (0, 0, 0)),
        ],
        out_specs=[pl.BlockSpec((2, rows, width), lambda i: (0, 0, 0))] * 2,
        out_shape=[shape((2, rows, width), BF16), shape((2, rows, width), F32)],
        scratch_shapes=[
            pltpu.VMEM((2, rows, pairs * rows), BF16),
            pltpu.VMEM((2, rows // 2, pairs * rows // 2), BF16),
            pltpu.VMEM((2, rows // 2, pairs * rows // 2), BF16),
        ],
        compiler_params=params(),
        cost_estimate=pl.CostEstimate(flops=4 * flops, bytes_accessed=2**21, transcendentals=0),
        name="key_side_kernel",
    )(bias, qd_group, stash)
    back = shifted(cross, "seq", -1)
    grad_queries = pl.pallas_call(
        functools.partial(late_query_kernel, scaling),
        grid=(1,),
        in_specs=[
            pl.BlockSpec(bias.shape, lambda i: (0, 0)),
            pl.BlockSpec(stash.shape, lambda i: (0, 0, 0)),
            pl.BlockSpec((late, 2, rows, width), lambda i: (groups // late - 1, 0, 0, 0)),
        ],
        out_specs=pl.BlockSpec((rows, groups, width), lambda i: (0, 0, 0)),
        out_shape=shape((rows, groups, width), BF16),
        scratch_shapes=[pltpu.VMEM((groups, rows, width), BF16)],
        compiler_params=params(),
        cost_estimate=pl.CostEstimate(flops=3 * flops, bytes_accessed=2**20, transcendentals=0),
        name="late_query_kernel",
    )(bias, stash, qd)
    grad_keys, grad_values = call(finish_kernel, (own, back), [shape((rows, width), BF16)] * 2)
    return (
        grad_queries.reshape(queries.shape),
        grad_keys.reshape(rows, 1, width),
        grad_values.reshape(rows, 1, width),
    )


def solution(mesh):
    placed = (
        P("seq", None, "tp", None),
        P("seq", None, None),
        P("seq", None, None),
        P("seq", None, "tp", None),
        P("seq", None, "tp"),
        P(),
    )
    return jax.shard_map(
        per_device,
        mesh=mesh,
        in_specs=placed,
        out_specs=(P("seq", None, "tp", None), P("seq", "tp", None), P("seq", "tp", None)),
        check_vma=False,
    )
```

```python
import functools
import math

import jax
import jax.numpy as jnp
from jax import lax
from jax.experimental import pallas as pl
from jax.experimental.pallas import tpu as pltpu
from jax.sharding import PartitionSpec as P

BF16 = jnp.bfloat16
F32 = jnp.float32
MASKED = -1e30
VMEM = pl.BlockSpec(memory_space=pltpu.VMEM)
HBM = pl.BlockSpec(memory_space=pl.ANY)


def params():
    return pltpu.CompilerParams(vmem_limit_bytes=16 * 1024 * 1024)


def dot_nt(a, b):
    return lax.dot_general(a, b, (((1,), (1,)), ((), ())), preferred_element_type=F32)


def dot_nn(a, b):
    return lax.dot_general(a, b, (((1,), (0,)), ((), ())), preferred_element_type=F32)


def shifted(block, axis, distance):
    size = lax.axis_size(axis)
    route = [(i - distance, i) for i in range(size) if 0 <= i - distance < size]
    return lax.ppermute(block, axis, route)


def fill_bias(bias, lengths_ref, first_row):
    keys, rows = bias.shape
    half = rows // 2
    docs = lengths_ref.shape[1]
    lengths = lengths_ref[...]
    i = lax.broadcasted_iota(jnp.int32, (docs, docs), 0)
    j = lax.broadcasted_iota(jnp.int32, (docs, docs), 1)
    ends = jnp.sum(jnp.where(j <= i, lengths, 0), axis=1, keepdims=True) - first_row
    t = lax.broadcasted_iota(jnp.int32, (docs, rows), 1)
    start = jnp.max(jnp.where(ends <= t, ends, -first_row), axis=0, keepdims=True)
    row = lax.broadcasted_iota(jnp.int32, (keys, rows), 0)
    t = lax.broadcasted_iota(jnp.int32, (keys, rows), 1)
    u = jnp.where((row >= rows) & (t < half), row - 2 * rows, row - half)
    bias[...] = jnp.where((u <= t) & (u >= start), 0.0, MASKED).astype(F32)


def window_dots(keys, queries):
    rows = queries.shape[0]
    half = rows // 2
    middle = dot_nt(keys[half : half + rows], queries)
    corners = jnp.concatenate(
        [dot_nt(keys[:half], queries[:half]), dot_nt(keys[half + rows :], queries[half:])], axis=1
    )
    return middle, corners


def pair_terms(query, dout, key, value, bias, scaling):
    rows = query.shape[0]
    fold = scaling * math.log2(math.e)
    middle, corners = window_dots(key, query)
    middle = middle * fold + bias[:rows]
    corners = corners * fold + bias[rows:]
    row_max = jnp.maximum(jnp.max(middle, axis=0, keepdims=True), jnp.max(corners, axis=0, keepdims=True))
    middle = jnp.exp2(middle - row_max)
    corners = jnp.exp2(corners - row_max)
    inverse = 1.0 / (jnp.sum(middle, axis=0, keepdims=True) + jnp.sum(corners, axis=0, keepdims=True))
    middle = middle * inverse
    corners = corners * inverse
    grad_middle, grad_corners = window_dots(value, dout)
    row_delta = jnp.sum(middle * grad_middle, axis=0, keepdims=True) + jnp.sum(
        corners * grad_corners, axis=0, keepdims=True
    )
    return (
        middle.astype(BF16),
        corners.astype(BF16),
        (middle * (grad_middle - row_delta)).astype(BF16),
        (corners * (grad_corners - row_delta)).astype(BF16),
    )


def query_prepare_kernel(exp_ref, query_ref, grad_ref, qd_ref):
    qd_ref[:, 0] = jnp.swapaxes(query_ref[...], 0, 1)
    blocks, groups = exp_ref.shape
    rows = grad_ref.shape[0] // blocks
    factor = jnp.exp2(exp_ref[...].astype(F32)).astype(BF16)
    for b in range(blocks):
        part = pl.ds(b * rows, rows)
        qd_ref[:, 1, part] = jnp.swapaxes(grad_ref[part], 0, 1) * factor[b][:, None, None]


def key_prepare_kernel(lengths_ref, key_ref, value_ref, kv_ref, bias_ref, bias):
    fill_bias(bias, lengths_ref, lax.axis_index("seq") * bias.shape[1])
    bias_ref[...] = bias[...].astype(BF16)
    kv_ref[0] = jnp.swapaxes(key_ref[...], 0, 1)
    kv_ref[1] = jnp.swapaxes(value_ref[...], 0, 1)


def query_grads(scaling, query, dout, key, value, bias):
    rows = query.shape[0]
    half = rows // 2
    _, _, middle, corners = pair_terms(query, dout, key, value, bias, scaling)
    key_t = key.T
    total = dot_nn(key_t[:, half : half + rows], middle) + jnp.concatenate(
        [dot_nn(key_t[:, :half], corners[:, :half]), dot_nn(key_t[:, half + rows :], corners[:, half:])],
        axis=1,
    )
    return (total * scaling).astype(BF16).T


def early_query_kernel(scaling, bias_ref, here_ref, kv_ref, qd_all_ref, stash_ref, qd_ref, done):
    d = lax.axis_index("tp")
    half = here_ref.shape[0] // 2
    first = (d & 1) * half
    late = half - first
    fetch = pltpu.make_async_copy(qd_all_ref.at[pl.ds(first, half)], qd_ref, done)
    fetch.start()
    bias = bias_ref[...].astype(F32)
    for i in range(2):
        stash_ref[2 * i] = here_ref[half * i + (d & (half - 1))]
        stash_ref[2 * i + 1] = kv_ref[i, d]
        for y in range(half):
            stash_ref[4 + half + 2 * y + i] = kv_ref[i, late + y]
    fetch.wait()
    for y in range(half):
        stash_ref[4 + y] = query_grads(
            scaling,
            qd_ref[y, 0],
            qd_ref[y, 1],
            jnp.concatenate([here_ref[y], kv_ref[0, first + y]], axis=0),
            jnp.concatenate([here_ref[half + y], kv_ref[1, first + y]], axis=0),
            bias,
        )


def late_query_kernel(scaling, bias_ref, other_ref, stash_ref, qd_ref, out_ref, grads, swapped, done):
    half = other_ref.shape[0] // 2
    first = (lax.axis_index("tp") & 1) * half
    late = half - first
    bias = bias_ref[...].astype(F32)
    for y in range(half):
        grads[first + y] = stash_ref[4 + y]
        at = 4 + half + 2 * y
        grads[late + y] = query_grads(
            scaling,
            qd_ref[y, 0],
            qd_ref[y, 1],
            jnp.concatenate([other_ref[y], stash_ref[at]], axis=0),
            jnp.concatenate([other_ref[half + y], stash_ref[at + 1]], axis=0),
            bias,
        )
    chunks = done.shape[0]
    rows = swapped.shape[0] // chunks
    copies = []
    for i in range(chunks):
        part = pl.ds(i * rows, rows)
        swapped[part] = jnp.swapaxes(grads[:, part], 0, 1)
        copies.append(pltpu.make_async_copy(swapped.at[part], out_ref.at[part], done.at[i]))
        copies[-1].start()
    for copy in copies:
        copy.wait()


def key_side_kernel(
    scaling, bias_ref, qd_ref, window_ref, other_ref, qd_here_ref, cross_ref, own_ref, late_ref, mid_terms, left_terms, right_terms, done
):
    heads, _, rows, width = qd_ref.shape
    half = rows // 2
    d = lax.axis_index("tp")
    count = other_ref.shape[0] // 2
    fetch = pltpu.make_async_copy(qd_here_ref.at[pl.ds((1 - (d & 1)) * count, count)], late_ref, done)
    fetch.start()
    came_here = (d >= count) == ((d & 1) == 1)
    back = [jnp.where(came_here, window_ref[2 * i], other_ref[count * i + (d & (count - 1))]) for i in range(2)]
    key = jnp.concatenate([back[0], window_ref[1]], axis=0)
    value = jnp.concatenate([back[1], window_ref[3]], axis=0)
    bias = bias_ref[...].astype(F32)
    for h in range(heads):
        probs, probs_c, grads, grads_c = pair_terms(qd_ref[h, 0], qd_ref[h, 1], key, value, bias, scaling)
        at, at_half = pl.ds(h * rows, rows), pl.ds(h * half, half)
        mid_terms[0, :, at] = grads
        mid_terms[1, :, at] = probs
        left_terms[0, :, at_half] = grads_c[:, :half]
        left_terms[1, :, at_half] = probs_c[:, :half]
        right_terms[0, :, at_half] = grads_c[:, half:]
        right_terms[1, :, at_half] = probs_c[:, half:]
    for i, factor in ((0, scaling), (1, 1.0)):
        both = qd_ref[:, i].reshape(heads * rows, width)
        early = qd_ref[:, i, :half].reshape(heads * half, width)
        late = qd_ref[:, i, half:].reshape(heads * half, width)
        middle = dot_nn(mid_terms[i], both) * factor
        cross_ref[i, :half] = (dot_nn(left_terms[i], early) * factor).astype(BF16)
        cross_ref[i, half:] = middle[:half].astype(BF16)
        own_ref[i, :half] = middle[half:]
        own_ref[i, half:] = dot_nn(right_terms[i], late) * factor
    fetch.wait()


def finish_kernel(own_ref, back_ref, key_ref, value_ref):
    key_ref[...] = (own_ref[0] + back_ref[0].astype(F32)).astype(BF16)
    value_ref[...] = (own_ref[1] + back_ref[1].astype(F32)).astype(BF16)


def per_device(queries, keys, values, grad_out, exponents, lengths):
    rows, groups, _, width = queries.shape
    scaling = width ** (-0.5)
    shape = jax.ShapeDtypeStruct
    device = lax.axis_index("tp")
    lengths = lengths.reshape(1, -1)
    pairs = 8
    flops = 2 * 2 * rows * rows * width * pairs

    def call(kernel, operands, out_shape, scratch=(), last=VMEM, out=VMEM, dots=0):
        many = isinstance(out_shape, list)
        return pl.pallas_call(
            kernel,
            in_specs=[VMEM] * (len(operands) - 1) + [last],
            out_specs=[out] * len(out_shape) if many else out,
            out_shape=out_shape,
            scratch_shapes=list(scratch),
            compiler_params=params(),
            cost_estimate=pl.CostEstimate(flops=flops * dots + 10**6, bytes_accessed=2**20, transcendentals=0),
            name=(kernel.func if isinstance(kernel, functools.partial) else kernel).__name__,
        )(*operands)

    half = groups // 2
    half_kv = [lax.dynamic_slice(block, (0, (device & 1) * half, 0), (rows, half, width)) for block in (keys, values)]
    half_kv = jnp.swapaxes(jnp.concatenate(half_kv, axis=1), 0, 1)
    exponents = exponents.reshape(-1, groups)
    here = shifted(half_kv, "seq", 1)
    queries, half_kv = lax.optimization_barrier((queries, half_kv))
    qd = call(
        query_prepare_kernel,
        (exponents, queries.reshape(rows, groups, width), grad_out.reshape(rows, groups, width)),
        shape((groups, 2, rows, width), BF16),
    )
    qd_group = lax.all_to_all(qd, "tp", split_axis=0, concat_axis=0, tiled=True)
    kv_shape = shape((2, groups, rows, width), BF16)
    bias_shape = (rows + rows // 2, rows)
    kv, bias = call(
        key_prepare_kernel,
        (lengths, keys, values),
        [kv_shape, shape(bias_shape, BF16)],
        [pltpu.VMEM(bias_shape, F32)],
        dots=20,
    )
    other = lax.ppermute(here, "tp", [(d, d ^ 1) for d in range(lax.axis_size("tp"))])
    fetch = [pltpu.VMEM((half, 2, rows, width), BF16), pltpu.SemaphoreType.DMA(())]
    stash = call(
        functools.partial(early_query_kernel, scaling),
        (bias, here, kv, qd),
        shape((4 + 3 * half, rows, width), BF16),
        fetch,
        last=HBM,
        dots=1,
    )
    cross, own, late_qd = call(
        functools.partial(key_side_kernel, scaling),
        (bias, qd_group, stash, other, qd),
        [shape((2, rows, width), BF16), shape((2, rows, width), F32), shape((half, 2, rows, width), BF16)],
        [
            pltpu.VMEM((2, rows, pairs * rows), BF16),
            pltpu.VMEM((2, rows // 2, pairs * rows // 2), BF16),
            pltpu.VMEM((2, rows // 2, pairs * rows // 2), BF16),
            pltpu.SemaphoreType.DMA(()),
        ],
        last=HBM,
        dots=4,
    )
    back = shifted(cross, "seq", -1)
    grad_queries = call(
        functools.partial(late_query_kernel, scaling),
        (bias, other, stash, late_qd),
        shape((rows, groups, width), BF16),
        [
            pltpu.VMEM((groups, rows, width), BF16),
            pltpu.VMEM((rows, groups, width), BF16),
            pltpu.SemaphoreType.DMA((4,)),
        ],
        out=HBM,
        dots=3,
    )
    grad_keys, grad_values = call(finish_kernel, (own, back), [shape((rows, width), BF16)] * 2)
    return (
        grad_queries.reshape(queries.shape),
        grad_keys.reshape(rows, 1, width),
        grad_values.reshape(rows, 1, width),
    )


def solution(mesh):
    placed = (
        P("seq", None, "tp", None),
        P("seq", None, None),
        P("seq", None, None),
        P("seq", None, "tp", None),
        P("seq", None, "tp"),
        P(),
    )
    return jax.shard_map(
        per_device,
        mesh=mesh,
        in_specs=placed,
        out_specs=(P("seq", None, "tp", None), P("seq", "tp", None), P("seq", "tp", None)),
        check_vma=False,
    )
```

```python
import functools
import math

import jax
import jax.numpy as jnp
from jax import lax
from jax.experimental import pallas as pl
from jax.experimental.pallas import tpu as pltpu
from jax.sharding import PartitionSpec as P

BF16 = jnp.bfloat16
F32 = jnp.float32
MASKED = -1e30
VMEM = pl.BlockSpec(memory_space=pltpu.VMEM)
HBM = pl.BlockSpec(memory_space=pl.ANY)


def params():
    return pltpu.CompilerParams(vmem_limit_bytes=16 * 1024 * 1024)


def dot_nt(a, b):
    return lax.dot_general(a, b, (((1,), (1,)), ((), ())), preferred_element_type=F32)


def dot_nn(a, b):
    return lax.dot_general(a, b, (((1,), (0,)), ((), ())), preferred_element_type=F32)


def shifted(block, axis, distance):
    size = lax.axis_size(axis)
    route = [(i - distance, i) for i in range(size) if 0 <= i - distance < size]
    return lax.ppermute(block, axis, route)


def fill_bias(bias, lengths_ref, first_row):
    keys, rows = bias.shape
    half = rows // 2
    docs = lengths_ref.shape[1]
    lengths = lengths_ref[...]
    i = lax.broadcasted_iota(jnp.int32, (docs, docs), 0)
    j = lax.broadcasted_iota(jnp.int32, (docs, docs), 1)
    ends = jnp.sum(jnp.where(j <= i, lengths, 0), axis=1, keepdims=True) - first_row
    t = lax.broadcasted_iota(jnp.int32, (docs, rows), 1)
    start = jnp.max(jnp.where(ends <= t, ends, -first_row), axis=0, keepdims=True)
    row = lax.broadcasted_iota(jnp.int32, (keys, rows), 0)
    t = lax.broadcasted_iota(jnp.int32, (keys, rows), 1)
    u = jnp.where((row >= rows) & (t < half), row - 2 * rows, row - half)
    bias[...] = jnp.where((u <= t) & (u >= start), 0.0, MASKED).astype(F32)


def window_dots(keys, queries):
    rows = queries.shape[0]
    half = rows // 2
    middle = dot_nt(keys[half : half + rows], queries)
    corners = jnp.concatenate(
        [dot_nt(keys[:half], queries[:half]), dot_nt(keys[half + rows :], queries[half:])], axis=1
    )
    return middle, corners


def pair_terms(query, dout, key, value, bias, scaling):
    rows = query.shape[0]
    fold = scaling * math.log2(math.e)
    middle, corners = window_dots(key, query)
    middle = middle * fold + bias[:rows]
    corners = corners * fold + bias[rows:]
    row_max = jnp.maximum(jnp.max(middle, axis=0, keepdims=True), jnp.max(corners, axis=0, keepdims=True))
    middle = jnp.exp2(middle - row_max)
    corners = jnp.exp2(corners - row_max)
    inverse = 1.0 / (jnp.sum(middle, axis=0, keepdims=True) + jnp.sum(corners, axis=0, keepdims=True))
    middle = middle * inverse
    corners = corners * inverse
    grad_middle, grad_corners = window_dots(value, dout)
    row_delta = jnp.sum(middle * grad_middle, axis=0, keepdims=True) + jnp.sum(
        corners * grad_corners, axis=0, keepdims=True
    )
    return (
        middle.astype(BF16),
        corners.astype(BF16),
        (middle * (grad_middle - row_delta)).astype(BF16),
        (corners * (grad_corners - row_delta)).astype(BF16),
    )


def query_prepare_kernel(exp_ref, query_ref, grad_ref, qd_ref):
    qd_ref[:, 0] = jnp.swapaxes(query_ref[...], 0, 1)
    blocks, groups = exp_ref.shape
    rows = grad_ref.shape[0] // blocks
    factor = jnp.exp2(exp_ref[...].astype(F32)).astype(BF16)
    for b in range(blocks):
        part = pl.ds(b * rows, rows)
        qd_ref[:, 1, part] = jnp.swapaxes(grad_ref[part], 0, 1) * factor[b][:, None, None]


def key_prepare_kernel(lengths_ref, key_ref, value_ref, kv_ref, bias_ref, bias):
    fill_bias(bias, lengths_ref, lax.axis_index("seq") * bias.shape[1])
    bias_ref[...] = bias[...].astype(BF16)
    kv_ref[0] = jnp.swapaxes(key_ref[...], 0, 1)
    kv_ref[1] = jnp.swapaxes(value_ref[...], 0, 1)


def query_grads(scaling, query, dout, key, value, bias):
    rows = query.shape[0]
    half = rows // 2
    _, _, middle, corners = pair_terms(query, dout, key, value, bias, scaling)
    key_t = key.T
    total = dot_nn(key_t[:, half : half + rows], middle) + jnp.concatenate(
        [dot_nn(key_t[:, :half], corners[:, :half]), dot_nn(key_t[:, half + rows :], corners[:, half:])],
        axis=1,
    )
    return (total * scaling).astype(BF16).T


def early_query_kernel(scaling, bias_ref, here_ref, kv_ref, qd_all_ref, out_ref, next_ref, qd_ref, done):
    half = here_ref.shape[0] // 2
    first = (lax.axis_index("tp") & 1) * half
    fetch = pltpu.make_async_copy(qd_all_ref.at[pl.ds(first, half)], qd_ref, done.at[0])
    fetch.start()
    fetch_next = pltpu.make_async_copy(qd_all_ref.at[pl.ds(half - first, next_ref.shape[0])], next_ref, done.at[1])
    fetch_next.start()
    bias = bias_ref[...].astype(F32)
    fetch.wait()
    for y in range(half):
        out_ref[y] = query_grads(
            scaling,
            qd_ref[y, 0],
            qd_ref[y, 1],
            jnp.concatenate([here_ref[y], kv_ref[0, first + y]], axis=0),
            jnp.concatenate([here_ref[half + y], kv_ref[1, first + y]], axis=0),
            bias,
        )
    fetch_next.wait()


def middle_query_kernel(scaling, bias_ref, here_ref, other_ref, kv_ref, early_ref, qd_ref, stash_ref):
    d = lax.axis_index("tp")
    half = here_ref.shape[0] // 2
    count = qd_ref.shape[0]
    late = half - (d & 1) * half
    bias = bias_ref[...].astype(F32)
    for i in range(2):
        at = half * i + (d & (half - 1))
        stash_ref[3 * i] = here_ref[at]
        stash_ref[3 * i + 1] = other_ref[at]
        stash_ref[3 * i + 2] = kv_ref[i, d]
        for y in range(count, half):
            at = 6 + half + count + 4 * (y - count) + 2 * i
            stash_ref[at] = other_ref[half * i + y]
            stash_ref[at + 1] = kv_ref[i, late + y]
    stash_ref[6 : 6 + half] = early_ref[...]
    for y in range(count):
        stash_ref[6 + half + y] = query_grads(
            scaling,
            qd_ref[y, 0],
            qd_ref[y, 1],
            jnp.concatenate([other_ref[y], kv_ref[0, late + y]], axis=0),
            jnp.concatenate([other_ref[half + y], kv_ref[1, late + y]], axis=0),
            bias,
        )


def late_query_kernel(scaling, bias_ref, stash_ref, qd_ref, out_ref, grads, swapped, done):
    groups, window, _ = grads.shape
    half, left = groups // 2, qd_ref.shape[0]
    first = (lax.axis_index("tp") & 1) * half
    late = half - first
    bias = bias_ref[...].astype(F32)
    for y in range(half):
        grads[first + y] = stash_ref[6 + y]
    for y in range(half - left):
        grads[late + y] = stash_ref[6 + half + y]
    for i in range(left):
        at = 6 + groups - left + 4 * i
        key = stash_ref[at : at + 2].reshape(2 * window, -1)
        value = stash_ref[at + 2 : at + 4].reshape(2 * window, -1)
        grads[late + half - left + i] = query_grads(scaling, qd_ref[i, 0], qd_ref[i, 1], key, value, bias)
    chunks = done.shape[0]
    rows = window // chunks
    copies = []
    for i in range(chunks):
        part = pl.ds(i * rows, rows)
        swapped[part] = jnp.swapaxes(grads[:, part], 0, 1)
        copies.append(pltpu.make_async_copy(swapped.at[part], out_ref.at[part], done.at[i]))
        copies[-1].start()
    for copy in copies:
        copy.wait()


def key_side_kernel(
    scaling, bias_ref, qd_ref, stash_ref, qd_here_ref, cross_ref, own_ref, late_ref, mid_terms, left_terms, right_terms, done
):
    heads, _, rows, width = qd_ref.shape
    half = rows // 2
    left = late_ref.shape[0]
    first = (heads // 2) * (1 - (lax.axis_index("tp") & 1)) + heads // 2 - left
    fetch = pltpu.make_async_copy(qd_here_ref.at[pl.ds(first, left)], late_ref, done)
    fetch.start()
    d = lax.axis_index("tp")
    came_here = (d >= heads // 2) == ((d & 1) == 1)
    key, value = (
        jnp.concatenate([jnp.where(came_here, stash_ref[at], stash_ref[at + 1]), stash_ref[at + 2]], axis=0)
        for at in (0, 3)
    )
    bias = bias_ref[...].astype(F32)
    for h in range(heads):
        probs, probs_c, grads, grads_c = pair_terms(qd_ref[h, 0], qd_ref[h, 1], key, value, bias, scaling)
        at, at_half = pl.ds(h * rows, rows), pl.ds(h * half, half)
        mid_terms[0, :, at] = grads
        mid_terms[1, :, at] = probs
        left_terms[0, :, at_half] = grads_c[:, :half]
        left_terms[1, :, at_half] = probs_c[:, :half]
        right_terms[0, :, at_half] = grads_c[:, half:]
        right_terms[1, :, at_half] = probs_c[:, half:]
    for i, factor in ((0, scaling), (1, 1.0)):
        both = qd_ref[:, i].reshape(heads * rows, width)
        early = qd_ref[:, i, :half].reshape(heads * half, width)
        late = qd_ref[:, i, half:].reshape(heads * half, width)
        middle = dot_nn(mid_terms[i], both) * factor
        cross_ref[i, :half] = (dot_nn(left_terms[i], early) * factor).astype(BF16)
        cross_ref[i, half:] = middle[:half].astype(BF16)
        own_ref[i, :half] = middle[half:]
        own_ref[i, half:] = dot_nn(right_terms[i], late) * factor
    fetch.wait()


def finish_kernel(own_ref, back_ref, key_ref, value_ref):
    key_ref[...] = (own_ref[0] + back_ref[0].astype(F32)).astype(BF16)
    value_ref[...] = (own_ref[1] + back_ref[1].astype(F32)).astype(BF16)


def per_device(queries, keys, values, grad_out, exponents, lengths):
    rows, groups, _, width = queries.shape
    scaling = width ** (-0.5)
    shape = jax.ShapeDtypeStruct
    device = lax.axis_index("tp")
    lengths = lengths.reshape(1, -1)
    pairs = 8
    flops = 2 * 2 * rows * rows * width * pairs

    def call(kernel, operands, out_shape, scratch=(), last=VMEM, out=VMEM, dots=0):
        many = isinstance(out_shape, list)
        return pl.pallas_call(
            kernel,
            in_specs=[VMEM] * (len(operands) - 1) + [last],
            out_specs=[out] * len(out_shape) if many else out,
            out_shape=out_shape,
            scratch_shapes=list(scratch),
            compiler_params=params(),
            cost_estimate=pl.CostEstimate(flops=flops * dots + 10**6, bytes_accessed=2**20, transcendentals=0),
            name=(kernel.func if isinstance(kernel, functools.partial) else kernel).__name__,
        )(*operands)

    half = groups // 2
    half_kv = [lax.dynamic_slice(block, (0, (device & 1) * half, 0), (rows, half, width)) for block in (keys, values)]
    half_kv = jnp.swapaxes(jnp.concatenate(half_kv, axis=1), 0, 1)
    exponents = exponents.reshape(-1, groups)
    here = shifted(half_kv, "seq", 1)
    queries, half_kv = lax.optimization_barrier((queries, half_kv))
    qd = call(
        query_prepare_kernel,
        (exponents, queries.reshape(rows, groups, width), grad_out.reshape(rows, groups, width)),
        shape((groups, 2, rows, width), BF16),
    )
    qd_group = lax.all_to_all(qd, "tp", split_axis=0, concat_axis=0, tiled=True)
    kv_shape = shape((2, groups, rows, width), BF16)
    bias_shape = (rows + rows // 2, rows)
    kv, bias = call(
        key_prepare_kernel,
        (lengths, keys, values),
        [kv_shape, shape(bias_shape, BF16)],
        [pltpu.VMEM(bias_shape, F32)],
        dots=20,
    )
    other = lax.ppermute(here, "tp", [(d, d ^ 1) for d in range(lax.axis_size("tp"))])
    middle = 2
    early, next_qd = call(
        functools.partial(early_query_kernel, scaling),
        (bias, here, kv, qd),
        [shape((half, rows, width), BF16), shape((middle, 2, rows, width), BF16)],
        [pltpu.VMEM((half, 2, rows, width), BF16), pltpu.SemaphoreType.DMA((2,))],
        last=HBM,
        dots=1,
    )
    stash = call(
        functools.partial(middle_query_kernel, scaling),
        (bias, here, other, kv, early, next_qd),
        shape((6 + half + middle + 4 * (half - middle), rows, width), BF16),
        dots=1,
    )
    cross, own, late_qd = call(
        functools.partial(key_side_kernel, scaling),
        (bias, qd_group, stash, qd),
        [shape((2, rows, width), BF16), shape((2, rows, width), F32), shape((half - middle, 2, rows, width), BF16)],
        [
            pltpu.VMEM((2, rows, pairs * rows), BF16),
            pltpu.VMEM((2, rows // 2, pairs * rows // 2), BF16),
            pltpu.VMEM((2, rows // 2, pairs * rows // 2), BF16),
            pltpu.SemaphoreType.DMA(()),
        ],
        last=HBM,
        dots=4,
    )
    back = shifted(cross, "seq", -1)
    grad_queries = call(
        functools.partial(late_query_kernel, scaling),
        (bias, stash, late_qd),
        shape((rows, groups, width), BF16),
        [
            pltpu.VMEM((groups, rows, width), BF16),
            pltpu.VMEM((rows, groups, width), BF16),
            pltpu.SemaphoreType.DMA((4,)),
        ],
        out=HBM,
        dots=3,
    )
    grad_keys, grad_values = call(finish_kernel, (own, back), [shape((rows, width), BF16)] * 2)
    return (
        grad_queries.reshape(queries.shape),
        grad_keys.reshape(rows, 1, width),
        grad_values.reshape(rows, 1, width),
    )


def solution(mesh):
    placed = (
        P("seq", None, "tp", None),
        P("seq", None, None),
        P("seq", None, None),
        P("seq", None, "tp", None),
        P("seq", None, "tp"),
        P(),
    )
    return jax.shard_map(
        per_device,
        mesh=mesh,
        in_specs=placed,
        out_specs=(P("seq", None, "tp", None), P("seq", "tp", None), P("seq", "tp", None)),
        check_vma=False,
    )
```

```python
import functools
import math

import jax
import jax.numpy as jnp
from jax import lax
from jax.experimental import pallas as pl
from jax.experimental.pallas import tpu as pltpu
from jax.sharding import PartitionSpec as P

BF16 = jnp.bfloat16
F32 = jnp.float32
MASKED = -1e30
VMEM = pl.BlockSpec(memory_space=pltpu.VMEM)
HBM = pl.BlockSpec(memory_space=pl.ANY)


def params():
    return pltpu.CompilerParams(vmem_limit_bytes=16 * 1024 * 1024)


def dot_nt(a, b):
    return lax.dot_general(a, b, (((1,), (1,)), ((), ())), preferred_element_type=F32)


def dot_nn(a, b):
    return lax.dot_general(a, b, (((1,), (0,)), ((), ())), preferred_element_type=F32)


def shifted(block, axis, distance):
    size = lax.axis_size(axis)
    route = [(i - distance, i) for i in range(size) if 0 <= i - distance < size]
    return lax.ppermute(block, axis, route)


def fill_bias(bias, lengths_ref, first_row):
    keys, rows = bias.shape
    half = rows // 2
    docs = lengths_ref.shape[1]
    lengths = lengths_ref[...]
    i = lax.broadcasted_iota(jnp.int32, (docs, docs), 0)
    j = lax.broadcasted_iota(jnp.int32, (docs, docs), 1)
    ends = jnp.sum(jnp.where(j <= i, lengths, 0), axis=1, keepdims=True) - first_row
    t = lax.broadcasted_iota(jnp.int32, (docs, rows), 1)
    start = jnp.max(jnp.where(ends <= t, ends, -first_row), axis=0, keepdims=True)
    row = lax.broadcasted_iota(jnp.int32, (keys, rows), 0)
    t = lax.broadcasted_iota(jnp.int32, (keys, rows), 1)
    u = jnp.where((row >= rows) & (t < half), row - 2 * rows, row - half)
    bias[...] = jnp.where((u <= t) & (u >= start), 0.0, MASKED).astype(F32)


def window_dots(keys, queries):
    rows = queries.shape[0]
    half = rows // 2
    middle = dot_nt(keys[half : half + rows], queries)
    corners = jnp.concatenate(
        [dot_nt(keys[:half], queries[:half]), dot_nt(keys[half + rows :], queries[half:])], axis=1
    )
    return middle, corners


def shifted_exps(query, key, bias, scaling):
    rows = query.shape[0]
    fold = scaling * math.log2(math.e)
    middle, corners = window_dots(key, query)
    middle = middle * fold + bias[:rows]
    corners = corners * fold + bias[rows:]
    row_max = jnp.maximum(jnp.max(middle, axis=0, keepdims=True), jnp.max(corners, axis=0, keepdims=True))
    middle = jnp.exp2(middle - row_max)
    corners = jnp.exp2(corners - row_max)
    total = jnp.sum(middle, axis=0, keepdims=True) + jnp.sum(corners, axis=0, keepdims=True)
    return middle, corners, 1.0 / total


def pair_terms(query, dout, key, value, bias, scaling):
    middle, corners, inverse = shifted_exps(query, key, bias, scaling)
    middle = middle * inverse
    corners = corners * inverse
    grad_middle, grad_corners = window_dots(value, dout)
    row_delta = jnp.sum(middle * grad_middle, axis=0, keepdims=True) + jnp.sum(
        corners * grad_corners, axis=0, keepdims=True
    )
    return (
        middle.astype(BF16),
        corners.astype(BF16),
        (middle * (grad_middle - row_delta)).astype(BF16),
        (corners * (grad_corners - row_delta)).astype(BF16),
    )


def query_prepare_kernel(exp_ref, query_ref, grad_ref, qd_ref):
    qd_ref[:, 0] = jnp.swapaxes(query_ref[...], 0, 1)
    blocks, groups = exp_ref.shape
    rows = grad_ref.shape[0] // blocks
    factor = jnp.exp2(exp_ref[...].astype(F32)).astype(BF16)
    for b in range(blocks):
        part = pl.ds(b * rows, rows)
        qd_ref[:, 1, part] = jnp.swapaxes(grad_ref[part], 0, 1) * factor[b][:, None, None]


def key_prepare_kernel(lengths_ref, key_ref, value_ref, qd_ref, kv_ref, bias_ref, half_ref, bias, done):
    half = half_ref.shape[0]
    fetch = pltpu.make_async_copy(qd_ref.at[pl.ds((lax.axis_index("tp") & 1) * half, half)], half_ref, done)
    fetch.start()
    fill_bias(bias, lengths_ref, lax.axis_index("seq") * bias.shape[1])
    bias_ref[...] = bias[...].astype(BF16)
    kv_ref[0] = jnp.swapaxes(key_ref[...], 0, 1)
    kv_ref[1] = jnp.swapaxes(value_ref[...], 0, 1)
    fetch.wait()


def query_grads(scaling, query, dout, key, value, bias):
    rows = query.shape[0]
    half = rows // 2
    middle, corners, inverse = shifted_exps(query, key, bias, scaling)
    grad_middle, grad_corners = window_dots(value, dout)
    row_delta = inverse * (
        jnp.sum(middle * grad_middle, axis=0, keepdims=True) + jnp.sum(corners * grad_corners, axis=0, keepdims=True)
    )
    middle = (middle * (grad_middle - row_delta)).astype(BF16)
    corners = (corners * (grad_corners - row_delta)).astype(BF16)
    key_t = key.T
    total = dot_nn(key_t[:, half : half + rows], middle) + jnp.concatenate(
        [dot_nn(key_t[:, :half], corners[:, :half]), dot_nn(key_t[:, half + rows :], corners[:, half:])],
        axis=1,
    )
    return (total * (inverse * scaling)).astype(BF16).T


def early_query_kernel(scaling, bias_ref, here_ref, kv_ref, qd_ref, qd_all_ref, out_ref, next_ref, done):
    half = here_ref.shape[0] // 2
    first = (lax.axis_index("tp") & 1) * half
    fetch = pltpu.make_async_copy(qd_all_ref.at[pl.ds(half - first, next_ref.shape[0])], next_ref, done)
    fetch.start()
    bias = bias_ref[...].astype(F32)
    for y in range(half):
        out_ref[y] = query_grads(
            scaling,
            qd_ref[y, 0],
            qd_ref[y, 1],
            jnp.concatenate([here_ref[y], kv_ref[0, first + y]], axis=0),
            jnp.concatenate([here_ref[half + y], kv_ref[1, first + y]], axis=0),
            bias,
        )
    fetch.wait()


def middle_query_kernel(scaling, bias_ref, here_ref, other_ref, kv_ref, early_ref, qd_ref, stash_ref):
    d = lax.axis_index("tp")
    half = here_ref.shape[0] // 2
    count = qd_ref.shape[0]
    late = half - (d & 1) * half
    bias = bias_ref[...].astype(F32)
    for i in range(2):
        at = half * i + (d & (half - 1))
        stash_ref[3 * i] = here_ref[at]
        stash_ref[3 * i + 1] = other_ref[at]
        stash_ref[3 * i + 2] = kv_ref[i, d]
        for y in range(count, half):
            at = 6 + half + count + 4 * (y - count) + 2 * i
            stash_ref[at] = other_ref[half * i + y]
            stash_ref[at + 1] = kv_ref[i, late + y]
    stash_ref[6 : 6 + half] = early_ref[...]
    for y in range(count):
        stash_ref[6 + half + y] = query_grads(
            scaling,
            qd_ref[y, 0],
            qd_ref[y, 1],
            jnp.concatenate([other_ref[y], kv_ref[0, late + y]], axis=0),
            jnp.concatenate([other_ref[half + y], kv_ref[1, late + y]], axis=0),
            bias,
        )


def late_query_kernel(scaling, bias_ref, stash_ref, qd_ref, out_ref, grads, swapped, done):
    groups, window, _ = grads.shape
    half, left = groups // 2, qd_ref.shape[0]
    first = (lax.axis_index("tp") & 1) * half
    late = half - first
    bias = bias_ref[...].astype(F32)
    for y in range(half):
        grads[first + y] = stash_ref[6 + y]
    for y in range(half - left):
        grads[late + y] = stash_ref[6 + half + y]
    for i in range(left):
        at = 6 + groups - left + 4 * i
        key = stash_ref[at : at + 2].reshape(2 * window, -1)
        value = stash_ref[at + 2 : at + 4].reshape(2 * window, -1)
        grads[late + half - left + i] = query_grads(scaling, qd_ref[i, 0], qd_ref[i, 1], key, value, bias)
    chunks = done.shape[0]
    rows = window // chunks
    copies = []
    for i in range(chunks):
        part = pl.ds(i * rows, rows)
        swapped[part] = jnp.swapaxes(grads[:, part], 0, 1)
        copies.append(pltpu.make_async_copy(swapped.at[part], out_ref.at[part], done.at[i]))
        copies[-1].start()
    for copy in copies:
        copy.wait()


def key_side_kernel(
    scaling, bias_ref, qd_ref, stash_ref, qd_here_ref, cross_ref, own_ref, late_ref, mid_terms, left_terms, right_terms, done
):
    heads, _, rows, width = qd_ref.shape
    half = rows // 2
    left = late_ref.shape[0]
    first = (heads // 2) * (1 - (lax.axis_index("tp") & 1)) + heads // 2 - left
    fetch = pltpu.make_async_copy(qd_here_ref.at[pl.ds(first, left)], late_ref, done)
    fetch.start()
    d = lax.axis_index("tp")
    came_here = (d >= heads // 2) == ((d & 1) == 1)
    key, value = (
        jnp.concatenate([jnp.where(came_here, stash_ref[at], stash_ref[at + 1]), stash_ref[at + 2]], axis=0)
        for at in (0, 3)
    )
    bias = bias_ref[...].astype(F32)
    for h in range(heads):
        probs, probs_c, grads, grads_c = pair_terms(qd_ref[h, 0], qd_ref[h, 1], key, value, bias, scaling)
        at, at_half = pl.ds(h * rows, rows), pl.ds(h * half, half)
        mid_terms[0, :, at] = grads
        mid_terms[1, :, at] = probs
        left_terms[0, :, at_half] = grads_c[:, :half]
        left_terms[1, :, at_half] = probs_c[:, :half]
        right_terms[0, :, at_half] = grads_c[:, half:]
        right_terms[1, :, at_half] = probs_c[:, half:]
    for i, factor in ((0, scaling), (1, 1.0)):
        both = qd_ref[:, i].reshape(heads * rows, width)
        early = qd_ref[:, i, :half].reshape(heads * half, width)
        late = qd_ref[:, i, half:].reshape(heads * half, width)
        middle = dot_nn(mid_terms[i], both) * factor
        cross_ref[i, :half] = (dot_nn(left_terms[i], early) * factor).astype(BF16)
        cross_ref[i, half:] = middle[:half].astype(BF16)
        own_ref[i, :half] = middle[half:]
        own_ref[i, half:] = dot_nn(right_terms[i], late) * factor
    fetch.wait()


def finish_kernel(own_ref, back_ref, key_ref, value_ref):
    key_ref[...] = (own_ref[0] + back_ref[0].astype(F32)).astype(BF16)
    value_ref[...] = (own_ref[1] + back_ref[1].astype(F32)).astype(BF16)


def per_device(queries, keys, values, grad_out, exponents, lengths):
    rows, groups, _, width = queries.shape
    scaling = width ** (-0.5)
    shape = jax.ShapeDtypeStruct
    device = lax.axis_index("tp")
    lengths = lengths.reshape(1, -1)
    pairs = 8
    flops = 2 * 2 * rows * rows * width * pairs

    def call(kernel, operands, out_shape, scratch=(), last=VMEM, out=VMEM, dots=0):
        many = isinstance(out_shape, list)
        return pl.pallas_call(
            kernel,
            in_specs=[VMEM] * (len(operands) - 1) + [last],
            out_specs=[out] * len(out_shape) if many else out,
            out_shape=out_shape,
            scratch_shapes=list(scratch),
            compiler_params=params(),
            cost_estimate=pl.CostEstimate(flops=flops * dots + 10**6, bytes_accessed=2**20, transcendentals=0),
            name=(kernel.func if isinstance(kernel, functools.partial) else kernel).__name__,
        )(*operands)

    half = groups // 2
    half_kv = [lax.dynamic_slice(block, (0, (device & 1) * half, 0), (rows, half, width)) for block in (keys, values)]
    half_kv = jnp.swapaxes(jnp.concatenate(half_kv, axis=1), 0, 1)
    exponents = exponents.reshape(-1, groups)
    here = shifted(half_kv, "seq", 1)
    queries, half_kv = lax.optimization_barrier((queries, half_kv))
    qd = call(
        query_prepare_kernel,
        (exponents, queries.reshape(rows, groups, width), grad_out.reshape(rows, groups, width)),
        shape((groups, 2, rows, width), BF16),
    )
    qd_group = lax.all_to_all(qd, "tp", split_axis=0, concat_axis=0, tiled=True)
    kv_shape = shape((2, groups, rows, width), BF16)
    bias_shape = (rows + rows // 2, rows)
    kv, bias, half_qd = call(
        key_prepare_kernel,
        (lengths, keys, values, qd),
        [kv_shape, shape(bias_shape, BF16), shape((half, 2, rows, width), BF16)],
        [pltpu.VMEM(bias_shape, F32), pltpu.SemaphoreType.DMA(())],
        last=HBM,
        dots=20,
    )
    other = lax.ppermute(here, "tp", [(d, d ^ 1) for d in range(lax.axis_size("tp"))])
    middle = 2
    early, next_qd = call(
        functools.partial(early_query_kernel, scaling),
        (bias, here, kv, half_qd, qd),
        [shape((half, rows, width), BF16), shape((middle, 2, rows, width), BF16)],
        [pltpu.SemaphoreType.DMA(())],
        last=HBM,
        dots=1,
    )
    stash = call(
        functools.partial(middle_query_kernel, scaling),
        (bias, here, other, kv, early, next_qd),
        shape((6 + half + middle + 4 * (half - middle), rows, width), BF16),
        dots=1,
    )
    cross, own, late_qd = call(
        functools.partial(key_side_kernel, scaling),
        (bias, qd_group, stash, qd),
        [shape((2, rows, width), BF16), shape((2, rows, width), F32), shape((half - middle, 2, rows, width), BF16)],
        [
            pltpu.VMEM((2, rows, pairs * rows), BF16),
            pltpu.VMEM((2, rows // 2, pairs * rows // 2), BF16),
            pltpu.VMEM((2, rows // 2, pairs * rows // 2), BF16),
            pltpu.SemaphoreType.DMA(()),
        ],
        last=HBM,
        dots=4,
    )
    back = shifted(cross, "seq", -1)
    grad_queries = call(
        functools.partial(late_query_kernel, scaling),
        (bias, stash, late_qd),
        shape((rows, groups, width), BF16),
        [
            pltpu.VMEM((groups, rows, width), BF16),
            pltpu.VMEM((rows, groups, width), BF16),
            pltpu.SemaphoreType.DMA((4,)),
        ],
        out=HBM,
        dots=3,
    )
    grad_keys, grad_values = call(finish_kernel, (own, back), [shape((rows, width), BF16)] * 2)
    return (
        grad_queries.reshape(queries.shape),
        grad_keys.reshape(rows, 1, width),
        grad_values.reshape(rows, 1, width),
    )


def solution(mesh):
    placed = (
        P("seq", None, "tp", None),
        P("seq", None, None),
        P("seq", None, None),
        P("seq", None, "tp", None),
        P("seq", None, "tp"),
        P(),
    )
    return jax.shard_map(
        per_device,
        mesh=mesh,
        in_specs=placed,
        out_specs=(P("seq", None, "tp", None), P("seq", "tp", None), P("seq", "tp", None)),
        check_vma=False,
    )
```

```python
import functools
import math

import jax
import jax.numpy as jnp
from jax import lax
from jax.experimental import pallas as pl
from jax.experimental.pallas import tpu as pltpu
from jax.sharding import PartitionSpec as P

BF16 = jnp.bfloat16
F32 = jnp.float32
MASKED = -1e30
VMEM = pl.BlockSpec(memory_space=pltpu.VMEM)
HBM = pl.BlockSpec(memory_space=pl.ANY)


def params():
    return pltpu.CompilerParams(vmem_limit_bytes=16 * 1024 * 1024)


def dot_nt(a, b):
    return lax.dot_general(a, b, (((1,), (1,)), ((), ())), preferred_element_type=F32)


def dot_nn(a, b):
    return lax.dot_general(a, b, (((1,), (0,)), ((), ())), preferred_element_type=F32)


def shifted(block, axis, distance):
    size = lax.axis_size(axis)
    route = [(i - distance, i) for i in range(size) if 0 <= i - distance < size]
    return lax.ppermute(block, axis, route)


def fill_bias(bias, lengths_ref, first_row):
    keys, rows = bias.shape
    half = rows // 2
    docs = lengths_ref.shape[1]
    lengths = lengths_ref[...]
    i = lax.broadcasted_iota(jnp.int32, (docs, docs), 0)
    j = lax.broadcasted_iota(jnp.int32, (docs, docs), 1)
    ends = jnp.sum(jnp.where(j <= i, lengths, 0), axis=1, keepdims=True) - first_row
    t = lax.broadcasted_iota(jnp.int32, (docs, rows), 1)
    start = jnp.max(jnp.where(ends <= t, ends, -first_row), axis=0, keepdims=True)
    row = lax.broadcasted_iota(jnp.int32, (keys, rows), 0)
    t = lax.broadcasted_iota(jnp.int32, (keys, rows), 1)
    u = jnp.where((row >= rows) & (t < half), row - 2 * rows, row - half)
    bias[...] = jnp.where((u <= t) & (u >= start), 0.0, MASKED).astype(F32)


def window_dots(keys, queries):
    rows = queries.shape[0]
    half = rows // 2
    middle = dot_nt(keys[half : half + rows], queries)
    corners = jnp.concatenate(
        [dot_nt(keys[:half], queries[:half]), dot_nt(keys[half + rows :], queries[half:])], axis=1
    )
    return middle, corners


def shifted_exps(query, key, bias, scaling):
    rows = query.shape[0]
    fold = scaling * math.log2(math.e)
    middle, corners = window_dots(key, query)
    middle = middle * fold + bias[:rows]
    corners = corners * fold + bias[rows:]
    row_max = jnp.maximum(jnp.max(middle, axis=0, keepdims=True), jnp.max(corners, axis=0, keepdims=True))
    middle = jnp.exp2(middle - row_max)
    corners = jnp.exp2(corners - row_max)
    total = jnp.sum(middle, axis=0, keepdims=True) + jnp.sum(corners, axis=0, keepdims=True)
    return middle, corners, 1.0 / total


def query_prepare_kernel(exp_ref, query_ref, grad_ref, out_ref, qd, done):
    blocks, groups = exp_ref.shape
    rows = grad_ref.shape[0] // blocks
    factor = jnp.exp2(exp_ref[...].astype(F32)).astype(BF16)
    copies = []
    for i, ref in enumerate((query_ref, grad_ref)):
        for b in range(blocks):
            part = pl.ds(b * rows, rows)
            piece = jnp.swapaxes(ref[part], 0, 1)
            qd[:, i, part] = piece * factor[b][:, None, None] if i else piece
            copies.append(
                pltpu.make_async_copy(qd.at[:, i, part], out_ref.at[:, i, part], done.at[i * blocks + b])
            )
            copies[-1].start()
    for copy in copies:
        copy.wait()


def key_prepare_kernel(lengths_ref, key_ref, value_ref, qd_ref, kv_ref, bias_ref, half_ref, bias, done):
    half = half_ref.shape[0]
    fetch = pltpu.make_async_copy(qd_ref.at[pl.ds((lax.axis_index("tp") & 1) * half, half)], half_ref, done)
    fetch.start()
    fill_bias(bias, lengths_ref, lax.axis_index("seq") * bias.shape[1])
    bias_ref[...] = bias[...].astype(BF16)
    kv_ref[0] = jnp.swapaxes(key_ref[...], 0, 1)
    kv_ref[1] = jnp.swapaxes(value_ref[...], 0, 1)
    fetch.wait()


def query_grads(scaling, query, dout, key, value, bias):
    rows = query.shape[0]
    half = rows // 2
    middle, corners, inverse = shifted_exps(query, key, bias, scaling)
    grad_middle, grad_corners = window_dots(value, dout)
    row_delta = inverse * (
        jnp.sum(middle * grad_middle, axis=0, keepdims=True) + jnp.sum(corners * grad_corners, axis=0, keepdims=True)
    )
    middle = (middle * (grad_middle - row_delta)).astype(BF16)
    corners = (corners * (grad_corners - row_delta)).astype(BF16)
    key_t = key.T
    total = dot_nn(key_t[:, half : half + rows], middle) + jnp.concatenate(
        [dot_nn(key_t[:, :half], corners[:, :half]), dot_nn(key_t[:, half + rows :], corners[:, half:])],
        axis=1,
    )
    return (total * (inverse * scaling)).astype(BF16).T


def early_query_kernel(scaling, bias_ref, here_ref, kv_ref, qd_ref, qd_all_ref, out_ref, next_ref, done):
    half = here_ref.shape[0] // 2
    first = (lax.axis_index("tp") & 1) * half
    fetch = pltpu.make_async_copy(qd_all_ref.at[pl.ds(half - first, next_ref.shape[0])], next_ref, done)
    fetch.start()
    bias = bias_ref[...].astype(F32)
    for y in range(half):
        out_ref[y] = query_grads(
            scaling,
            qd_ref[y, 0],
            qd_ref[y, 1],
            jnp.concatenate([here_ref[y], kv_ref[0, first + y]], axis=0),
            jnp.concatenate([here_ref[half + y], kv_ref[1, first + y]], axis=0),
            bias,
        )
    fetch.wait()


def middle_query_kernel(scaling, bias_ref, here_ref, other_ref, kv_ref, early_ref, qd_ref, stash_ref):
    d = lax.axis_index("tp")
    half = here_ref.shape[0] // 2
    count = qd_ref.shape[0]
    late = half - (d & 1) * half
    bias = bias_ref[...].astype(F32)
    for i in range(2):
        at = half * i + (d & (half - 1))
        stash_ref[3 * i] = here_ref[at]
        stash_ref[3 * i + 1] = other_ref[at]
        stash_ref[3 * i + 2] = kv_ref[i, d]
        for y in range(count, half):
            at = 6 + half + count + 4 * (y - count) + 2 * i
            stash_ref[at] = other_ref[half * i + y]
            stash_ref[at + 1] = kv_ref[i, late + y]
    stash_ref[6 : 6 + half] = early_ref[...]
    for y in range(count):
        stash_ref[6 + half + y] = query_grads(
            scaling,
            qd_ref[y, 0],
            qd_ref[y, 1],
            jnp.concatenate([other_ref[y], kv_ref[0, late + y]], axis=0),
            jnp.concatenate([other_ref[half + y], kv_ref[1, late + y]], axis=0),
            bias,
        )


def late_query_kernel(scaling, bias_ref, stash_ref, qd_ref, out_ref, grads, swapped, done):
    groups, window, _ = grads.shape
    half, left = groups // 2, qd_ref.shape[0]
    first = (lax.axis_index("tp") & 1) * half
    late = half - first
    bias = bias_ref[...].astype(F32)
    for y in range(half):
        grads[first + y] = stash_ref[6 + y]
    for y in range(half - left):
        grads[late + y] = stash_ref[6 + half + y]
    for i in range(left):
        at = 6 + groups - left + 4 * i
        key = stash_ref[at : at + 2].reshape(2 * window, -1)
        value = stash_ref[at + 2 : at + 4].reshape(2 * window, -1)
        grads[late + half - left + i] = query_grads(scaling, qd_ref[i, 0], qd_ref[i, 1], key, value, bias)
    chunks = done.shape[0]
    rows = window // chunks
    copies = []
    for i in range(chunks):
        part = pl.ds(i * rows, rows)
        swapped[part] = jnp.swapaxes(grads[:, part], 0, 1)
        copies.append(pltpu.make_async_copy(swapped.at[part], out_ref.at[part], done.at[i]))
        copies[-1].start()
    for copy in copies:
        copy.wait()


def key_side_kernel(
    scaling, bias_ref, qd_ref, stash_ref, qd_here_ref, cross_ref, own_ref, late_ref, terms, done
):
    heads, _, rows, width = qd_ref.shape
    half = rows // 2
    left = late_ref.shape[0]
    first = (heads // 2) * (1 - (lax.axis_index("tp") & 1)) + heads // 2 - left
    fetch = pltpu.make_async_copy(qd_here_ref.at[pl.ds(first, left)], late_ref, done)
    fetch.start()
    d = lax.axis_index("tp")
    came_here = (d >= heads // 2) == ((d & 1) == 1)
    key, value = (
        jnp.concatenate([jnp.where(came_here, stash_ref[at], stash_ref[at + 1]), stash_ref[at + 2]], axis=0)
        for at in (0, 3)
    )
    for second in range(2):
        lanes = slice(second * half, (second + 1) * half)
        reach = slice(second * half, (second + 3) * half)
        middle, corner = bias_ref[:rows, lanes], bias_ref[rows:, lanes]
        bias = jnp.concatenate([middle, corner] if second else [corner, middle], axis=0).astype(F32)
        bias = jnp.concatenate([bias, bias], axis=1)
        for h in range(0, heads, 2):
            query = qd_ref[h : h + 2, 0, lanes].reshape(rows, width)
            dout = qd_ref[h : h + 2, 1, lanes].reshape(rows, width)
            scores = dot_nt(key[reach], query) * (scaling * math.log2(math.e)) + bias
            shifted_exp = jnp.exp2(scores - jnp.max(scores, axis=0, keepdims=True))
            probs = shifted_exp * (1.0 / jnp.sum(shifted_exp, axis=0, keepdims=True))
            grad_probs = dot_nt(value[reach], dout)
            row_delta = jnp.sum(probs * grad_probs, axis=0, keepdims=True)
            at = pl.ds(h * half, rows)
            terms[second, 0, :, at] = (probs * (grad_probs - row_delta)).astype(BF16)
            terms[second, 1, :, at] = probs.astype(BF16)
    for i, factor in ((0, scaling), (1, 1.0)):
        first, last = (
            dot_nn(terms[second, i], qd_ref[:, i, second * half : (second + 1) * half].reshape(heads * half, width)) * factor
            for second in range(2)
        )
        cross_ref[i, :half] = first[:half].astype(BF16)
        cross_ref[i, half:] = (first[half:rows] + last[:half]).astype(BF16)
        own_ref[i, :half] = first[rows:] + last[half:rows]
        own_ref[i, half:] = last[rows:]
    fetch.wait()


def finish_kernel(own_ref, back_ref, key_ref, value_ref):
    key_ref[...] = (own_ref[0] + back_ref[0].astype(F32)).astype(BF16)
    value_ref[...] = (own_ref[1] + back_ref[1].astype(F32)).astype(BF16)


def per_device(queries, keys, values, grad_out, exponents, lengths):
    rows, groups, _, width = queries.shape
    scaling = width ** (-0.5)
    shape = jax.ShapeDtypeStruct
    device = lax.axis_index("tp")
    lengths = lengths.reshape(1, -1)
    pairs = 8
    flops = 2 * 2 * rows * rows * width * pairs

    def call(kernel, operands, out_shape, scratch=(), last=VMEM, out=VMEM, dots=0):
        many = isinstance(out_shape, list)
        return pl.pallas_call(
            kernel,
            in_specs=[VMEM] * (len(operands) - 1) + [last],
            out_specs=[out] * len(out_shape) if many else out,
            out_shape=out_shape,
            scratch_shapes=list(scratch),
            compiler_params=params(),
            cost_estimate=pl.CostEstimate(flops=flops * dots + 10**6, bytes_accessed=2**20, transcendentals=0),
            name=(kernel.func if isinstance(kernel, functools.partial) else kernel).__name__,
        )(*operands)

    half = groups // 2
    half_kv = [lax.dynamic_slice(block, (0, (device & 1) * half, 0), (rows, half, width)) for block in (keys, values)]
    half_kv = jnp.swapaxes(jnp.concatenate(half_kv, axis=1), 0, 1)
    exponents = exponents.reshape(-1, groups)
    here = shifted(half_kv, "seq", 1)
    queries, half_kv = lax.optimization_barrier((queries, half_kv))
    qd_shape = (groups, 2, rows, width)
    qd = call(
        query_prepare_kernel,
        (exponents, queries.reshape(rows, groups, width), grad_out.reshape(rows, groups, width)),
        shape(qd_shape, BF16),
        [pltpu.VMEM(qd_shape, BF16), pltpu.SemaphoreType.DMA((2 * exponents.shape[0],))],
        out=HBM,
    )
    qd_group = lax.all_to_all(qd, "tp", split_axis=0, concat_axis=0, tiled=True)
    kv_shape = shape((2, groups, rows, width), BF16)
    bias_shape = (rows + rows // 2, rows)
    kv, bias, half_qd = call(
        key_prepare_kernel,
        (lengths, keys, values, qd),
        [kv_shape, shape(bias_shape, BF16), shape((half, 2, rows, width), BF16)],
        [pltpu.VMEM(bias_shape, F32), pltpu.SemaphoreType.DMA(())],
        last=HBM,
        dots=20,
    )
    other = lax.ppermute(here, "tp", [(d, d ^ 1) for d in range(lax.axis_size("tp"))])
    middle = 2
    early, next_qd = call(
        functools.partial(early_query_kernel, scaling),
        (bias, here, kv, half_qd, qd),
        [shape((half, rows, width), BF16), shape((middle, 2, rows, width), BF16)],
        [pltpu.SemaphoreType.DMA(())],
        last=HBM,
        dots=1,
    )
    stash = call(
        functools.partial(middle_query_kernel, scaling),
        (bias, here, other, kv, early, next_qd),
        shape((6 + half + middle + 4 * (half - middle), rows, width), BF16),
        dots=1,
    )
    cross, own, late_qd = call(
        functools.partial(key_side_kernel, scaling),
        (bias, qd_group, stash, qd),
        [shape((2, rows, width), BF16), shape((2, rows, width), F32), shape((half - middle, 2, rows, width), BF16)],
        [
            pltpu.VMEM((2, 2, rows + rows // 2, pairs * rows // 2), BF16),
            pltpu.SemaphoreType.DMA(()),
        ],
        last=HBM,
        dots=4,
    )
    back = shifted(cross, "seq", -1)
    grad_queries = call(
        functools.partial(late_query_kernel, scaling),
        (bias, stash, late_qd),
        shape((rows, groups, width), BF16),
        [
            pltpu.VMEM((groups, rows, width), BF16),
            pltpu.VMEM((rows, groups, width), BF16),
            pltpu.SemaphoreType.DMA((4,)),
        ],
        out=HBM,
        dots=3,
    )
    grad_keys, grad_values = call(finish_kernel, (own, back), [shape((rows, width), BF16)] * 2)
    return (
        grad_queries.reshape(queries.shape),
        grad_keys.reshape(rows, 1, width),
        grad_values.reshape(rows, 1, width),
    )


def solution(mesh):
    placed = (
        P("seq", None, "tp", None),
        P("seq", None, None),
        P("seq", None, None),
        P("seq", None, "tp", None),
        P("seq", None, "tp"),
        P(),
    )
    return jax.shard_map(
        per_device,
        mesh=mesh,
        in_specs=placed,
        out_specs=(P("seq", None, "tp", None), P("seq", "tp", None), P("seq", "tp", None)),
        check_vma=False,
    )
```

```python
import functools
import math

import jax
import jax.numpy as jnp
from jax import lax
from jax.experimental import pallas as pl
from jax.experimental.pallas import tpu as pltpu
from jax.sharding import PartitionSpec as P

BF16 = jnp.bfloat16
F32 = jnp.float32
MASKED = -1e30
VMEM = pl.BlockSpec(memory_space=pltpu.VMEM)
HBM = pl.BlockSpec(memory_space=pl.ANY)


def params():
    return pltpu.CompilerParams(vmem_limit_bytes=16 * 1024 * 1024)


def dot_nt(a, b):
    return lax.dot_general(a, b, (((1,), (1,)), ((), ())), preferred_element_type=F32)


def dot_nn(a, b):
    return lax.dot_general(a, b, (((1,), (0,)), ((), ())), preferred_element_type=F32)


def shifted(block, axis, distance):
    size = lax.axis_size(axis)
    route = [(i - distance, i) for i in range(size) if 0 <= i - distance < size]
    return lax.ppermute(block, axis, route)


def fill_bias(bias, lengths_ref, first_row):
    keys, rows = bias.shape
    half = rows // 2
    docs = lengths_ref.shape[1]
    lengths = lengths_ref[...]
    i = lax.broadcasted_iota(jnp.int32, (docs, docs), 0)
    j = lax.broadcasted_iota(jnp.int32, (docs, docs), 1)
    ends = jnp.sum(jnp.where(j <= i, lengths, 0), axis=1, keepdims=True) - first_row
    t = lax.broadcasted_iota(jnp.int32, (docs, rows), 1)
    start = jnp.max(jnp.where(ends <= t, ends, -first_row), axis=0, keepdims=True)
    row = lax.broadcasted_iota(jnp.int32, (keys, rows), 0)
    t = lax.broadcasted_iota(jnp.int32, (keys, rows), 1)
    u = jnp.where((row >= rows) & (t < half), row - 2 * rows, row - half)
    bias[...] = jnp.where((u <= t) & (u >= start), 0.0, MASKED).astype(F32)


def window_dots(keys, queries):
    rows = queries.shape[0]
    half = rows // 2
    middle = dot_nt(keys[half : half + rows], queries)
    corners = jnp.concatenate(
        [dot_nt(keys[:half], queries[:half]), dot_nt(keys[half + rows :], queries[half:])], axis=1
    )
    return middle, corners


def shifted_exps(query, key, bias, scaling):
    rows = query.shape[0]
    fold = scaling * math.log2(math.e)
    middle, corners = window_dots(key, query)
    middle = middle * fold + bias[:rows]
    corners = corners * fold + bias[rows:]
    row_max = jnp.maximum(jnp.max(middle, axis=0, keepdims=True), jnp.max(corners, axis=0, keepdims=True))
    middle = jnp.exp2(middle - row_max)
    corners = jnp.exp2(corners - row_max)
    total = jnp.sum(middle, axis=0, keepdims=True) + jnp.sum(corners, axis=0, keepdims=True)
    return middle, corners, 1.0 / total


def query_prepare_kernel(exp_ref, query_ref, grad_ref, out_ref, qd, done):
    blocks, groups = exp_ref.shape
    rows = grad_ref.shape[0] // blocks
    factor = jnp.exp2(exp_ref[...].astype(F32)).astype(BF16)
    copies = []
    for i, ref in enumerate((query_ref, grad_ref)):
        for b in range(blocks):
            part = pl.ds(b * rows, rows)
            piece = jnp.swapaxes(ref[part], 0, 1)
            qd[:, i, part] = piece * factor[b][:, None, None] if i else piece
            copies.append(
                pltpu.make_async_copy(qd.at[:, i, part], out_ref.at[:, i, part], done.at[i * blocks + b])
            )
            copies[-1].start()
    for copy in copies:
        copy.wait()


def key_prepare_kernel(lengths_ref, key_ref, value_ref, qd_ref, kv_ref, bias_ref, half_ref, bias, done):
    half = half_ref.shape[0]
    fetch = pltpu.make_async_copy(qd_ref.at[pl.ds((lax.axis_index("tp") & 1) * half, half)], half_ref, done)
    fetch.start()
    fill_bias(bias, lengths_ref, lax.axis_index("seq") * bias.shape[1])
    bias_ref[...] = bias[...].astype(BF16)
    kv_ref[0] = jnp.swapaxes(key_ref[...], 0, 1)
    kv_ref[1] = jnp.swapaxes(value_ref[...], 0, 1)
    fetch.wait()


def query_grads(scaling, query, dout, key, value, bias):
    rows = query.shape[0]
    half = rows // 2
    middle, corners, inverse = shifted_exps(query, key, bias, scaling)
    grad_middle, grad_corners = window_dots(value, dout)
    row_delta = inverse * (
        jnp.sum(middle * grad_middle, axis=0, keepdims=True) + jnp.sum(corners * grad_corners, axis=0, keepdims=True)
    )
    middle = (middle * (grad_middle - row_delta)).astype(BF16)
    corners = (corners * (grad_corners - row_delta)).astype(BF16)
    key_t = key.T
    total = dot_nn(key_t[:, half : half + rows], middle) + jnp.concatenate(
        [dot_nn(key_t[:, :half], corners[:, :half]), dot_nn(key_t[:, half + rows :], corners[:, half:])],
        axis=1,
    )
    return (total * (inverse * scaling)).astype(BF16).T


def early_query_kernel(scaling, bias_ref, here_ref, kv_ref, qd_ref, qd_all_ref, out_ref, next_ref, done):
    half = here_ref.shape[0] // 2
    first = (lax.axis_index("tp") & 1) * half
    fetch = pltpu.make_async_copy(qd_all_ref.at[pl.ds(half - first, next_ref.shape[0])], next_ref, done)
    fetch.start()
    bias = bias_ref[...].astype(F32)
    for y in range(half):
        out_ref[y] = query_grads(
            scaling,
            qd_ref[y, 0],
            qd_ref[y, 1],
            jnp.concatenate([here_ref[y], kv_ref[0, first + y]], axis=0),
            jnp.concatenate([here_ref[half + y], kv_ref[1, first + y]], axis=0),
            bias,
        )
    fetch.wait()


def middle_query_kernel(scaling, bias_ref, here_ref, other_ref, kv_ref, early_ref, qd_ref, stash_ref):
    d = lax.axis_index("tp")
    half = here_ref.shape[0] // 2
    count = qd_ref.shape[0]
    late = half - (d & 1) * half
    bias = bias_ref[...].astype(F32)
    for i in range(2):
        at = half * i + (d & (half - 1))
        stash_ref[3 * i] = here_ref[at]
        stash_ref[3 * i + 1] = other_ref[at]
        stash_ref[3 * i + 2] = kv_ref[i, d]
        for y in range(count, half):
            at = 6 + half + count + 4 * (y - count) + 2 * i
            stash_ref[at] = other_ref[half * i + y]
            stash_ref[at + 1] = kv_ref[i, late + y]
    stash_ref[6 : 6 + half] = early_ref[...]
    for y in range(count):
        stash_ref[6 + half + y] = query_grads(
            scaling,
            qd_ref[y, 0],
            qd_ref[y, 1],
            jnp.concatenate([other_ref[y], kv_ref[0, late + y]], axis=0),
            jnp.concatenate([other_ref[half + y], kv_ref[1, late + y]], axis=0),
            bias,
        )


def late_query_kernel(scaling, bias_ref, stash_ref, qd_ref, out_ref, grads, swapped, done):
    groups, window, _ = grads.shape
    half, left = groups // 2, qd_ref.shape[0]
    first = (lax.axis_index("tp") & 1) * half
    late = half - first
    bias = bias_ref[...].astype(F32)
    for y in range(half):
        grads[first + y] = stash_ref[6 + y]
    for y in range(half - left):
        grads[late + y] = stash_ref[6 + half + y]
    for i in range(left):
        at = 6 + groups - left + 4 * i
        key = stash_ref[at : at + 2].reshape(2 * window, -1)
        value = stash_ref[at + 2 : at + 4].reshape(2 * window, -1)
        grads[late + half - left + i] = query_grads(scaling, qd_ref[i, 0], qd_ref[i, 1], key, value, bias)
    chunks = done.shape[0]
    rows = window // chunks
    copies = []
    for i in range(chunks):
        part = pl.ds(i * rows, rows)
        swapped[part] = jnp.swapaxes(grads[:, part], 0, 1)
        copies.append(pltpu.make_async_copy(swapped.at[part], out_ref.at[part], done.at[i]))
        copies[-1].start()
    for copy in copies:
        copy.wait()


def key_side_kernel(
    scaling, bias_ref, qd_ref, stash_ref, qd_here_ref, cross_ref, own_ref, late_ref, terms, done
):
    heads, _, rows, width = qd_ref.shape
    half = rows // 2
    left = late_ref.shape[0]
    first = (heads // 2) * (1 - (lax.axis_index("tp") & 1)) + heads // 2 - left
    fetch = pltpu.make_async_copy(qd_here_ref.at[pl.ds(first, left)], late_ref, done)
    fetch.start()
    d = lax.axis_index("tp")
    came_here = (d >= heads // 2) == ((d & 1) == 1)
    key, value = (
        jnp.concatenate([jnp.where(came_here, stash_ref[at], stash_ref[at + 1]), stash_ref[at + 2]], axis=0)
        for at in (0, 3)
    )
    for second in range(2):
        lanes = slice(second * half, (second + 1) * half)
        reach = slice(second * half, (second + 3) * half)
        middle, corner = bias_ref[:rows, lanes], bias_ref[rows:, lanes]
        bias = jnp.concatenate([middle, corner] if second else [corner, middle], axis=0).astype(F32)
        bias = jnp.concatenate([bias] * 4, axis=1)
        for h in range(0, heads, 4):
            query = qd_ref[h : h + 4, 0, lanes].reshape(2 * rows, width)
            dout = qd_ref[h : h + 4, 1, lanes].reshape(2 * rows, width)
            scores = dot_nt(key[reach], query) * (scaling * math.log2(math.e)) + bias
            shifted_exp = jnp.exp2(scores - jnp.max(scores, axis=0, keepdims=True))
            probs = shifted_exp * (1.0 / jnp.sum(shifted_exp, axis=0, keepdims=True))
            grad_probs = dot_nt(value[reach], dout)
            row_delta = jnp.sum(probs * grad_probs, axis=0, keepdims=True)
            at = pl.ds(h * half, 2 * rows)
            terms[second, 0, :, at] = (probs * (grad_probs - row_delta)).astype(BF16)
            terms[second, 1, :, at] = probs.astype(BF16)
    for i, factor in ((0, scaling), (1, 1.0)):
        first, last = (
            dot_nn(terms[second, i], qd_ref[:, i, second * half : (second + 1) * half].reshape(heads * half, width)) * factor
            for second in range(2)
        )
        cross_ref[i, :half] = first[:half].astype(BF16)
        cross_ref[i, half:] = (first[half:rows] + last[:half]).astype(BF16)
        own_ref[i, :half] = first[rows:] + last[half:rows]
        own_ref[i, half:] = last[rows:]
    fetch.wait()


def finish_kernel(own_ref, back_ref, key_ref, value_ref):
    key_ref[...] = (own_ref[0] + back_ref[0].astype(F32)).astype(BF16)
    value_ref[...] = (own_ref[1] + back_ref[1].astype(F32)).astype(BF16)


def per_device(queries, keys, values, grad_out, exponents, lengths):
    rows, groups, _, width = queries.shape
    scaling = width ** (-0.5)
    shape = jax.ShapeDtypeStruct
    device = lax.axis_index("tp")
    lengths = lengths.reshape(1, -1)
    pairs = 8
    flops = 2 * 2 * rows * rows * width * pairs

    def call(kernel, operands, out_shape, scratch=(), last=VMEM, out=VMEM, dots=0):
        many = isinstance(out_shape, list)
        return pl.pallas_call(
            kernel,
            in_specs=[VMEM] * (len(operands) - 1) + [last],
            out_specs=[out] * len(out_shape) if many else out,
            out_shape=out_shape,
            scratch_shapes=list(scratch),
            compiler_params=params(),
            cost_estimate=pl.CostEstimate(flops=flops * dots + 10**6, bytes_accessed=2**20, transcendentals=0),
            name=(kernel.func if isinstance(kernel, functools.partial) else kernel).__name__,
        )(*operands)

    half = groups // 2
    half_kv = [lax.dynamic_slice(block, (0, (device & 1) * half, 0), (rows, half, width)) for block in (keys, values)]
    half_kv = jnp.swapaxes(jnp.concatenate(half_kv, axis=1), 0, 1)
    exponents = exponents.reshape(-1, groups)
    here = shifted(half_kv, "seq", 1)
    queries, half_kv = lax.optimization_barrier((queries, half_kv))
    qd_shape = (groups, 2, rows, width)
    qd = call(
        query_prepare_kernel,
        (exponents, queries.reshape(rows, groups, width), grad_out.reshape(rows, groups, width)),
        shape(qd_shape, BF16),
        [pltpu.VMEM(qd_shape, BF16), pltpu.SemaphoreType.DMA((2 * exponents.shape[0],))],
        out=HBM,
    )
    qd_group = lax.all_to_all(qd, "tp", split_axis=0, concat_axis=0, tiled=True)
    kv_shape = shape((2, groups, rows, width), BF16)
    bias_shape = (rows + rows // 2, rows)
    kv, bias, half_qd = call(
        key_prepare_kernel,
        (lengths, keys, values, qd),
        [kv_shape, shape(bias_shape, BF16), shape((half, 2, rows, width), BF16)],
        [pltpu.VMEM(bias_shape, F32), pltpu.SemaphoreType.DMA(())],
        last=HBM,
        dots=20,
    )
    other = lax.ppermute(here, "tp", [(d, d ^ 1) for d in range(lax.axis_size("tp"))])
    middle = 2
    early, next_qd = call(
        functools.partial(early_query_kernel, scaling),
        (bias, here, kv, half_qd, qd),
        [shape((half, rows, width), BF16), shape((middle, 2, rows, width), BF16)],
        [pltpu.SemaphoreType.DMA(())],
        last=HBM,
        dots=1,
    )
    stash = call(
        functools.partial(middle_query_kernel, scaling),
        (bias, here, other, kv, early, next_qd),
        shape((6 + half + middle + 4 * (half - middle), rows, width), BF16),
        dots=1,
    )
    cross, own, late_qd = call(
        functools.partial(key_side_kernel, scaling),
        (bias, qd_group, stash, qd),
        [shape((2, rows, width), BF16), shape((2, rows, width), F32), shape((half - middle, 2, rows, width), BF16)],
        [
            pltpu.VMEM((2, 2, rows + rows // 2, pairs * rows // 2), BF16),
            pltpu.SemaphoreType.DMA(()),
        ],
        last=HBM,
        dots=4,
    )
    back = shifted(cross, "seq", -1)
    grad_queries = call(
        functools.partial(late_query_kernel, scaling),
        (bias, stash, late_qd),
        shape((rows, groups, width), BF16),
        [
            pltpu.VMEM((groups, rows, width), BF16),
            pltpu.VMEM((rows, groups, width), BF16),
            pltpu.SemaphoreType.DMA((4,)),
        ],
        out=HBM,
        dots=3,
    )
    grad_keys, grad_values = call(finish_kernel, (own, back), [shape((rows, width), BF16)] * 2)
    return (
        grad_queries.reshape(queries.shape),
        grad_keys.reshape(rows, 1, width),
        grad_values.reshape(rows, 1, width),
    )


def solution(mesh):
    placed = (
        P("seq", None, "tp", None),
        P("seq", None, None),
        P("seq", None, None),
        P("seq", None, "tp", None),
        P("seq", None, "tp"),
        P(),
    )
    return jax.shard_map(
        per_device,
        mesh=mesh,
        in_specs=placed,
        out_specs=(P("seq", None, "tp", None), P("seq", "tp", None), P("seq", "tp", None)),
        check_vma=False,
    )
```
